256 devices in a mesh: leaf: 16 (over z, x_lo), chan: 16 (over y, x_hi, core).
Axes of the slice: x: 4 (x_hi: 2, x_lo: 2; x = x_hi * 2 + x_lo), y: 4, z: 8, core: 2. Of those that a mesh axis runs over, the one named last changes fastest.
Arguments:
- features: float32 [512, 32, 512], P('chan', 'leaf'), may hold values from -6 to 6
- leaf_counts: int32 [16], P('leaf'), may hold values from 1 to 2, as said below
- occupancy: int32 [32, 512], P('leaf'), may hold values 0 or 1
- neighbours: int32 [32, 26], P('leaf'), may hold values from -1 to 31, as said below
- weight_in: float32 [27, 512, 512], P(None, 'chan'), may hold values from -0.0625 to 0.0625
- bias_in: float32 [512], P('chan'), may hold values from -3 to 3
- weight_out: float32 [27, 512, 512], P(None, 'chan'), may hold values from -0.125 to 0.125
- bias_out: float32 [512], P('chan'), may hold values from -3 to 3
Outputs:
- result: float32 [512, 32, 512], P('chan', 'leaf')
The draws below stay inside these ranges and needn't reach their ends.
Inputs may be any that keep to these rules, and one draw needn't show every extreme that they name: `leaf_counts`: each index of leaf has 1 to 2 live slots, and some index has all 2. `neighbours`: entries name live slots only, and dead slots have -1 in every column; the leaves sit on a grid, so a leaf's neighbour in a direction has that leaf as its neighbour in the opposite one.
All inputs are finite; a program needn't handle non-finite values. No bound on the sum of `occupancy` on one device may be relied on, other than what follows from the above.
Results may differ from the reference program's by a relative error of at most 0.0003.
Values sent between devices are 32-bit elements; how exact they have to be, the bound alone decides.
No kernel may reach another device: no remote copies, remote signals or barrier semaphores. Data moves between devices by JAX's collectives and lax.ppermute only.
A program may use at most 64 MiB of HBM per device.

```python
import jax
import jax.numpy as jnp
from jax import lax

C = 512
VOX = 512
SLOTS = 2
LEAVES = 32


DIRECTIONS = [(first, second, third) for first in (-1, 0, 1) for second in (-1, 0, 1) for third in (-1, 0, 1) if (first, second, third) != (0, 0, 0)]


def layout(key):
    devices = LEAVES // SLOTS
    key_count, key_full, key_cells = jax.random.split(key, 3)
    counts = jax.random.randint(key_count, (devices,), 1, SLOTS + 1)
    fullest = jax.random.randint(key_full, (), 0, devices)
    counts = jnp.where(jnp.arange(devices) == fullest, SLOTS, counts).astype(jnp.int32)
    live = (jnp.arange(SLOTS)[None, :] < counts[:, None]).reshape(LEAVES)
    ranking = jnp.cumsum(live.astype(jnp.int32)) - 1
    cells = jax.random.permutation(key_cells, 2 * LEAVES)
    placed = jnp.where(live, cells[jnp.maximum(ranking, 0)], 2 * LEAVES)
    table = jnp.full((2 * LEAVES + 1,), -1, jnp.int32).at[placed].set(jnp.arange(LEAVES, dtype=jnp.int32))
    table = table.at[2 * LEAVES].set(-1)
    depth = LEAVES // 8
    coord_x = placed // (4 * depth)
    coord_y = placed // depth % 4
    coord_z = placed % depth
    listed = []
    for offsets in DIRECTIONS:
        next_x = coord_x + offsets[0]
        next_y = coord_y + offsets[1]
        next_z = coord_z + offsets[2]
        inside = (next_x >= 0) & (next_x < 4) & (next_y >= 0) & (next_y < 4) & (next_z >= 0) & (next_z < depth) & live
        target = jnp.where(inside, (next_x * 4 + next_y) * depth + next_z, 2 * LEAVES)
        listed.append(table[target])
    return (counts, jnp.stack(listed, axis=1).astype(jnp.int32))


def draw_leaf_counts(key, part):
    counts, listed = layout(key)
    return counts


def draw_neighbours(key, part):
    counts, listed = layout(key)
    return listed


def set_ends(drawn, rng, smallest, largest):
    shape = drawn.shape
    index_at = [jax.random.randint(jax.random.fold_in(rng, axis), (), 0, shape[axis]) for axis in range(len(shape))]
    drawn = drawn.at[tuple(index_at)].set(smallest)
    longest = shape.index(max(shape))
    index_at[longest] = (index_at[longest] + 1) % shape[longest]
    return drawn.at[tuple(index_at)].set(largest)


def with_spikes(result, own_key, source, target, parts, factor):
    owner, partner = [(jnp.arange(result.shape[dim]) // (result.shape[dim] // parts)).reshape([-1 if axis == dim else 1 for axis in range(result.ndim)]) for dim in (source, target)]
    chosen = jax.random.permutation(own_key, parts)[partner]
    strong = (owner == chosen) | (owner == (partner + parts // 2) % parts)
    return jnp.where(strong, factor * result, result)


def block_scale(stream_key, shape, cuts, smallest, high):
    loudness, own = 1.0, jax.random.fold_in(stream_key, 6)
    for axis_at, parts in cuts:
        steps = jnp.exp(jax.random.uniform(jax.random.fold_in(own, axis_at), (parts,), jnp.float32, smallest / len(cuts), high / len(cuts)))
        loudness = loudness * jnp.repeat(steps, shape[axis_at] // parts).reshape([-1 if axis == axis_at else 1 for axis in range(len(shape))])
    return loudness


def scatter_about(rng, extent, scale, bound, shards=(), kind=jnp.bfloat16):
    entries = jax.random.normal(rng, extent, jnp.float32) * scale
    if len(shards) > 0:
        entries = block_scale(rng, extent, shards, -0.22, 0.18) * entries
    return jnp.clip(entries, min=-bound, max=bound).astype(kind)


def noise_with(rng, dims, width, reach, cuts, heavy, kind=jnp.bfloat16):
    array = width * jax.random.normal(rng, dims, jnp.float32)
    if cuts:
        array = array * block_scale(rng, dims, cuts, -0.22, 0.18)
    return jnp.clip(with_spikes(array, jax.random.fold_in(rng, 3), *heavy), -reach, reach).astype(kind)


def setup_inputs(seed: int = 0) -> dict:
    key_list = jax.random.split(jax.random.key(seed), 9)
    return {
        "features": scatter_about(key_list[0], (C, LEAVES, VOX), 1.0, 6.0, ((0, 16), (1, 16)), jnp.float32),
        "leaf_counts": draw_leaf_counts(jax.random.fold_in(key_list[8], 71), 0),
        "occupancy": set_ends((jax.random.randint(key_list[2], (LEAVES, VOX), 0, 4) < 3).astype(jnp.int32), jax.random.fold_in(key_list[2], 1), 0, 1),
        "neighbours": draw_neighbours(jax.random.fold_in(key_list[8], 71), 0),
        "weight_in": noise_with(key_list[4], (27, C, C), (27 * C) ** -0.5, 0.0625, ((1, 16),), (1, 2, 16, 2.0), jnp.float32),
        "bias_in": scatter_about(key_list[5], (C,), 0.5, 3.0, ((0, 16),), jnp.float32),
        "weight_out": noise_with(key_list[6], (27, C, C), (27 * C // 4) ** -0.5, 0.125, ((1, 16),), (1, 2, 16, 2.0), jnp.float32),
        "bias_out": scatter_about(key_list[7], (C,), 0.5, 3.0, ((0, 16),), jnp.float32),
    }


DIRECTIONS = [(first, second, third) for first in (-1, 0, 1) for second in (-1, 0, 1) for third in (-1, 0, 1) if (first, second, third) != (0, 0, 0)]


def source_range(offset):
    if offset < 0:
        return slice(7, 8)
    if offset > 0:
        return slice(0, 1)
    return slice(0, 8)


def target_range(offset):
    if offset < 0:
        return slice(0, 1)
    if offset > 0:
        return slice(9, 10)
    return slice(1, 9)


def pad_blocks(blocks, neighbours):
    padded = jnp.zeros(blocks.shape[:2] + (10, 10, 10), jnp.float32)
    padded = padded.at[:, :, 1:9, 1:9, 1:9].set(blocks)
    for number, offsets in enumerate(DIRECTIONS):
        column = neighbours[:, number]
        present = (column >= 0).astype(jnp.float32)
        fetched = jnp.take(blocks, jnp.maximum(column, 0), axis=1)
        ranges = tuple(source_range(offset) for offset in offsets)
        rim = fetched[(slice(None), slice(None)) + ranges] * present[None, :, None, None, None]
        places = tuple(target_range(offset) for offset in offsets)
        padded = padded.at[(slice(None), slice(None)) + places].set(rim)
    return padded


def convolve(blocks, neighbours, weight):
    padded = pad_blocks(blocks, neighbours)

    def single(block):
        columns = jnp.stack([block[:, shift_x:shift_x + 8, shift_y:shift_y + 8, shift_z:shift_z + 8].reshape(block.shape[0], VOX)
                             for shift_x in range(3) for shift_y in range(3) for shift_z in range(3)])
        return jnp.einsum("tio,tiv->ov", weight, columns, precision=lax.Precision.HIGHEST)

    outcome = lax.map(single, jnp.moveaxis(padded, 1, 0))
    return jnp.moveaxis(outcome, 0, 1)


def reference(features, leaf_counts, occupancy, neighbours, weight_in, bias_in, weight_out, bias_out):
    live = (jnp.arange(SLOTS, dtype=jnp.int32)[None, :] < leaf_counts[:, None]).reshape(LEAVES).astype(jnp.float32)
    active = occupancy.astype(jnp.float32) * live[:, None]
    inputs = (features * active[None]).reshape(C, LEAVES, 8, 8, 8)
    first = convolve(inputs, neighbours, weight_in)
    hidden = jnp.maximum(first + bias_in[:, None, None], 0.0) * active[None]
    second = convolve(hidden.reshape(C, LEAVES, 8, 8, 8), neighbours, weight_out)
    return (second + bias_out[:, None, None]) * active[None]
```

```python
import functools

import jax
import jax.numpy as jnp
from jax import lax
from jax.experimental import pallas as pl
from jax.experimental.pallas import tpu as pltpu
from jax.sharding import PartitionSpec as P

DIRECTIONS = [
    (first, second, third)
    for first in (-1, 0, 1)
    for second in (-1, 0, 1)
    for third in (-1, 0, 1)
    if (first, second, third) != (0, 0, 0)
]
VMEM = pl.BlockSpec(memory_space=pltpu.VMEM)
SMEM = pl.BlockSpec(memory_space=pltpu.SMEM)
F32 = jnp.float32
BF16 = jnp.bfloat16
ROWS = 24


def call(kernel, outs, scratch=(), flops=1000000, touched=1000000):
    return functools.partial(
        pl.pallas_call,
        kernel,
        out_shape=outs,
        scratch_shapes=list(scratch),
        compiler_params=pltpu.CompilerParams(vmem_limit_bytes=56 * 1024 * 1024),
        cost_estimate=pl.CostEstimate(flops=flops, bytes_accessed=touched, transcendentals=0),
    )


def arr(shape, dtype=F32):
    return jax.ShapeDtypeStruct(shape, dtype)


def weights_kernel(place, own, other, high, low):
    core = place[0]

    def step(tap, carry):
        mine = own[tap, :, pl.ds(pl.multiple_of(core * 256, 256), 256)]
        theirs = other[tap]
        first = jnp.where(core == 0, mine, theirs)
        second = jnp.where(core == 0, theirs, mine)
        both = jnp.concatenate([first, second], axis=0)
        top = both.astype(BF16)
        high[tap] = top
        low[tap] = (both - top.astype(F32)).astype(BF16)
        return carry

    lax.fori_loop(0, 27, step, 0)


def split_weights(place, own, other):
    outs = (arr((27, 64, 256), BF16), arr((27, 64, 256), BF16))
    return call(weights_kernel, outs, flops=4000000, touched=4500000)(
        in_specs=[SMEM, VMEM, VMEM], out_specs=(VMEM, VMEM)
    )(place, own, other)


def cut_faces(core, rows, faces):
    base = pl.multiple_of(core * 512, 512)
    faces[0:64, :] = jnp.concatenate([rows[pl.ds(base, 64), :], rows[pl.ds(base + 448, 64), :]], axis=1)
    for x in range(8):
        faces[64 + 8 * x : 72 + 8 * x, :] = jnp.concatenate(
            [rows[pl.ds(base + 64 * x, 8), :], rows[pl.ds(base + 64 * x + 56, 8), :]], axis=1
        )
    faces[128:192, :] = jnp.concatenate(
        [rows[pl.ds(base, 64, stride=8), :], rows[pl.ds(base + 7, 64, stride=8), :]], axis=1
    )


def features_kernel(place, counts, occupancy, own, other, rows, faces):
    core = place[0]
    for slot in range(2):
        active = occupancy[slot : slot + 1, :].astype(F32) * jnp.where(slot < counts[0], 1.0, 0.0)
        mine, theirs = own[:, slot, :], other[:, slot, :]
        first = jnp.where(core == 0, mine, theirs)
        second = jnp.where(core == 0, theirs, mine)
        both = jnp.concatenate([first, second], axis=0) * active
        rows[slot * 512 : slot * 512 + 512, :] = both.T
    cut_faces(core, rows, faces)


def hidden_kernel(place, own, other, rows, faces):
    core = place[0]
    for slot in range(2):
        mine, theirs = own[:, slot * 512 : slot * 512 + 512], other[:, slot * 512 : slot * 512 + 512]
        first = jnp.where(core == 0, mine, theirs)
        second = jnp.where(core == 0, theirs, mine)
        rows[slot * 512 : slot * 512 + 512, :] = jnp.concatenate([first, second], axis=0).T
    cut_faces(core, rows, faces)


def fill_rims(slot, place, neighbours, gathered, padded):
    core, low_x, depth = place[0], place[1], place[2]

    def at(x, y):
        return (x * 10 + y) * ROWS

    for number, (a, b, c) in enumerate(DIRECTIONS):
        entry = neighbours[slot, number]
        there = entry >= 0
        found = jnp.clip(entry, 0, 31)
        index = (
            ((found & 1) ^ core) * 16
            + ((depth - (found >> 2)) & 7) * 2
            + (((found >> 1) & 1) ^ low_x)
        )

        lead = 0 if a else (1 if b else 2)
        side = 64 if (a, b, c)[lead] < 0 else 0

        def load(where):
            value = gathered[index, where, :]
            return jnp.where(there, value[:, side : side + 64], 0.0)

        px, py = {-1: 0, 1: 9}.get(a), {-1: 0, 1: 9}.get(b)
        row = {-1: 7, 1: 16}.get(c)
        y_at, z_at = (7 if b < 0 else 0), (7 if c < 0 else 0)
        if lead == 0:
            if b == 0 and c == 0:
                face = load(pl.ds(0, 64))
                for y in range(8):
                    padded[pl.ds(at(px, 1 + y) + 8, 8), :] = face[8 * y : 8 * y + 8]
            elif c == 0:
                padded[pl.ds(at(px, py) + 8, 8), :] = load(pl.ds(8 * y_at, 8))
            elif b == 0:
                padded[pl.ds(at(px, 1) + row, 8, stride=ROWS), :] = load(pl.ds(z_at, 8, stride=8))
            else:
                padded[pl.ds(at(px, py) + row, 1), :] = load(pl.ds(8 * y_at + z_at, 1))
        elif lead == 1:
            if c == 0:
                face = load(pl.ds(64, 64))
                for x in range(8):
                    padded[pl.ds(at(1 + x, py) + 8, 8), :] = face[8 * x : 8 * x + 8]
            else:
                padded[pl.ds(at(1, py) + row, 8, stride=10 * ROWS), :] = load(pl.ds(64 + z_at, 8, stride=8))
        else:
            face = load(pl.ds(128, 64))
            for x in range(8):
                padded[pl.ds(at(1 + x, 1) + row, 8, stride=ROWS), :] = face[8 * x : 8 * x + 8]


def conv_kernel(place, neighbours, rows, *rest):
    blocks = rest[:16]
    high, low = rest[16:18]
    outs = rest[18:26]
    gathered, padded, columns, total, turned = rest[26:]
    for number in range(16):
        gathered[2 * number] = blocks[number][0]
        gathered[2 * number + 1] = blocks[number][1]
    for slot in range(2):
        for x in range(8):
            for y in range(8):
                padded[pl.ds(((1 + x) * 10 + 1 + y) * ROWS + 8, 8), :] = rows[
                    pl.ds(slot * 512 + x * 64 + y * 8, 8), :
                ]
        fill_rims(slot, place, neighbours, gathered, padded)
        for spot in range(100):
            before = padded[pl.ds(spot * ROWS + 7, 8), :]
            same = padded[pl.ds(spot * ROWS + 8, 8), :]
            after = padded[pl.ds(spot * ROWS + 9, 8), :]
            columns[spot // 10, spot % 10, :, 0:128] = jnp.concatenate([before, same], axis=1)
            columns[spot // 10, spot % 10, :, 128:192] = after

        for p in range(3):
            sums = None
            for q in range(3):
                values = columns[p : p + 8, q : q + 8, :, 0:192].reshape(512, 192)
                top = values.astype(BF16)
                rest_of = (values - top.astype(F32)).astype(BF16)
                tap = 9 * p + 3 * q
                heavy = high[tap : tap + 3].reshape(192, 256)
                light = low[tap : tap + 3].reshape(192, 256)
                dot = functools.partial(jnp.dot, preferred_element_type=F32)
                part = dot(top, heavy) + (dot(rest_of, heavy) + dot(top, light))
                sums = part if sums is None else sums + part
            if p == 0:
                total[...] = sums
            else:
                total[...] += sums
        turned[:, slot * 512 : slot * 512 + 512] = total[...].T
    chip = place[3]
    for step in range(8):
        outs[step][...] = turned[pl.ds(pl.multiple_of((chip ^ step) * 32, 32), 32), :]


def conv(place, neighbours, rows, blocks, high, low):
    outs = tuple(arr((32, 1024)) for _ in range(8))
    scratch = [
        pltpu.VMEM((32, 192, 128), F32),
        pltpu.VMEM((100 * ROWS, 64), F32),
        pltpu.VMEM((10, 10, 8, 256), F32),
        pltpu.VMEM((512, 256), F32),
        pltpu.VMEM((256, 1024), F32),
    ]
    return call(conv_kernel, outs, scratch, flops=2 * 3 * 1024 * 1728 * 256, touched=8000000)(
        in_specs=[SMEM, SMEM] + [VMEM] * 19, out_specs=tuple([VMEM] * 8)
    )(place, neighbours, rows, *blocks, high, low)


def finish_kernel(last, counts, occupancy, bias, *rest):
    parts, out = rest[:8], rest[8]
    value = parts[0][...]
    for part in parts[1:]:
        value = value + part[...]
    value = value + bias[...]
    if not last:
        value = jnp.maximum(value, 0.0)
    for slot in range(2):
        active = occupancy[slot : slot + 1, :].astype(F32) * jnp.where(slot < counts[0], 1.0, 0.0)
        piece = value[:, slot * 512 : slot * 512 + 512] * active
        if last:
            out[:, slot, :] = piece
        else:
            out[:, slot * 512 : slot * 512 + 512] = piece


def finish(last, counts, occupancy, bias, parts):
    out = arr((32, 2, 512) if last else (32, 1024))
    return call(functools.partial(finish_kernel, last), out, touched=1500000)(
        in_specs=[SMEM, VMEM, VMEM] + [VMEM] * 8, out_specs=VMEM
    )(counts, occupancy, bias.reshape(32, 1), *parts)


def to_other_core(value):
    return lax.ppermute(value, "chan", [(i, i ^ 1) for i in range(16)])


def gather_faces(faces):
    beside = lax.ppermute(faces, "leaf", [(i, i ^ 1) for i in range(16)])
    start = jnp.stack([faces, beside])
    found = [start] + [None] * 7
    up = down = start
    for step in range(1, 5):
        up = lax.ppermute(up, "leaf", [(i, (i + 2) % 16) for i in range(16)])
        found[step] = up
        if step < 4:
            down = lax.ppermute(down, "leaf", [(i, (i - 2) % 16) for i in range(16)])
            found[8 - step] = down
    return found + [to_other_core(block) for block in found]


def add_over_chips(parts):
    landed = []
    for step in range(8):
        pairs = [(2 * k + h, 8 * h + (k ^ step)) for k in range(8) for h in range(2)]
        landed.append(lax.ppermute(parts[step], "chan", pairs))
    return landed


def body(features, leaf_counts, occupancy, neighbours, weight_in, bias_in, weight_out, bias_out):
    leaf, chan = lax.axis_index("leaf"), lax.axis_index("chan")
    core = chan % 2
    place = jnp.stack([core, leaf % 2, leaf // 2, chan // 2]).astype(jnp.int32)
    others = to_other_core(features)
    rows, faces = call(features_kernel, (arr((1024, 64)), arr((192, 128))))(
        in_specs=[SMEM, SMEM, VMEM, VMEM, VMEM], out_specs=(VMEM, VMEM)
    )(place, leaf_counts, occupancy, features, others)

    def exchanged(weight):
        given = lax.dynamic_slice_in_dim(weight, (1 - core) * 256, 256, 2)
        return split_weights(place, weight, to_other_core(given))

    blocks = gather_faces(faces)
    high, low = exchanged(weight_in)
    high_out, low_out = exchanged(weight_out)
    parts = conv(place, neighbours, rows, blocks, high, low)
    hidden = finish(False, leaf_counts, occupancy, bias_in, add_over_chips(parts))
    rows, faces = call(hidden_kernel, (arr((1024, 64)), arr((192, 128))))(
        in_specs=[SMEM, VMEM, VMEM], out_specs=(VMEM, VMEM)
    )(place, hidden, to_other_core(hidden))
    blocks = gather_faces(faces)
    parts = conv(place, neighbours, rows, blocks, high_out, low_out)
    return finish(True, leaf_counts, occupancy, bias_out, add_over_chips(parts))


def solution(mesh):
    placed = (
        P("chan", "leaf", None),
        P("leaf"),
        P("leaf", None),
        P("leaf", None),
        P(None, "chan", None),
        P("chan"),
        P(None, "chan", None),
        P("chan"),
    )
    return jax.shard_map(
        body, mesh=mesh, in_specs=placed, out_specs=P("chan", "leaf", None), check_vma=False
    )
```

```python
import functools

import jax
import jax.numpy as jnp
from jax import lax
from jax.experimental import pallas as pl
from jax.experimental.pallas import tpu as pltpu
from jax.sharding import PartitionSpec as P

DIRECTIONS = [
    (first, second, third)
    for first in (-1, 0, 1)
    for second in (-1, 0, 1)
    for third in (-1, 0, 1)
    if (first, second, third) != (0, 0, 0)
]
VMEM = pl.BlockSpec(memory_space=pltpu.VMEM)
SMEM = pl.BlockSpec(memory_space=pltpu.SMEM)
F32 = jnp.float32
BF16 = jnp.bfloat16
ROWS = 24


def call(kernel, outs, scratch=(), flops=1000000, touched=1000000):
    return functools.partial(
        pl.pallas_call,
        kernel,
        out_shape=outs,
        scratch_shapes=list(scratch),
        compiler_params=pltpu.CompilerParams(vmem_limit_bytes=56 * 1024 * 1024),
        cost_estimate=pl.CostEstimate(flops=flops, bytes_accessed=touched, transcendentals=0),
    )


def arr(shape, dtype=F32):
    return jax.ShapeDtypeStruct(shape, dtype)


def weights_kernel(place, own, other, high, low):
    core = place[0]

    def step(tap, carry):
        mine, theirs = own[tap], other[tap]
        first = jnp.where(core == 0, mine, theirs)
        second = jnp.where(core == 0, theirs, mine)
        both = jnp.concatenate([first, second], axis=0)
        top = both.astype(BF16)
        high[tap] = top
        low[tap] = (both - top.astype(F32)).astype(BF16)
        return carry

    lax.fori_loop(0, 27, step, 0)


def split_weights(place, own, other):
    outs = (arr((27, 64, 512), BF16), arr((27, 64, 512), BF16))
    return call(weights_kernel, outs, flops=8000000, touched=9000000)(
        in_specs=[SMEM, VMEM, VMEM], out_specs=(VMEM, VMEM)
    )(place, own, other)


def cut_faces(rows, faces):
    faces[0:64, :] = jnp.concatenate([rows[0:64, :], rows[448:512, :]], axis=1)
    for x in range(8):
        faces[64 + 8 * x : 72 + 8 * x, :] = jnp.concatenate(
            [rows[64 * x : 64 * x + 8, :], rows[64 * x + 56 : 64 * x + 64, :]], axis=1
        )
    faces[128:192, :] = jnp.concatenate(
        [rows[pl.ds(0, 64, stride=8), :], rows[pl.ds(7, 64, stride=8), :]], axis=1
    )


def in_order(core, own, other):
    first = jnp.where(core == 0, own, other)
    second = jnp.where(core == 0, other, own)
    return jnp.concatenate([first, second], axis=0)


def active_voxels(core, counts, occupancy):
    chosen = jnp.where(core == 0, occupancy[0:1, :], occupancy[1:2, :]).astype(F32)
    return chosen * jnp.where(core < counts[0], 1.0, 0.0)


def features_kernel(place, counts, occupancy, own, other, rows, faces):
    core = place[0]
    mine = jnp.where(core == 0, own[:, 0, :], own[:, 1, :])
    both = in_order(core, mine, other[...])
    rows[...] = (both * active_voxels(core, counts, occupancy)).T
    cut_faces(rows, faces)


def added(core, own_bias, other_bias, parts):
    value = parts[0][...]
    for part in parts[1:]:
        value = value + part[...]
    return value + in_order(core, own_bias[...], other_bias[...])


def hidden_kernel(place, counts, occupancy, own_bias, other_bias, *rest):
    core = place[0]
    rows, faces = rest[8:]
    value = jnp.maximum(added(core, own_bias, other_bias, rest[:8]), 0.0)
    rows[...] = (value * active_voxels(core, counts, occupancy)).T
    cut_faces(rows, faces)


def result_kernel(place, counts, occupancy, own_bias, other_bias, *rest):
    core = place[0]
    keep, give = rest[8:]
    value = added(core, own_bias, other_bias, rest[:8]) * active_voxels(core, counts, occupancy)
    keep[...] = jnp.where(core == 0, value[0:32], value[32:64])
    give[...] = jnp.where(core == 0, value[32:64], value[0:32])


def merge_kernel(place, keep, got, out):
    core = place[0]
    out[:, 0, :] = jnp.where(core == 0, keep[...], got[...])
    out[:, 1, :] = jnp.where(core == 0, got[...], keep[...])


def fill_rims(place, neighbours, gathered, padded):
    core, low_x, depth = place[0], place[1], place[2]

    def at(x, y):
        return (x * 10 + y) * ROWS

    for number, (a, b, c) in enumerate(DIRECTIONS):
        entry = neighbours[place[0], number]
        there = entry >= 0
        found = jnp.clip(entry, 0, 31)
        index = (
            ((found & 1) ^ core) * 16
            + ((depth - (found >> 2)) & 7) * 2
            + (((found >> 1) & 1) ^ low_x)
        )

        lead = 0 if a else (1 if b else 2)
        side = 64 if (a, b, c)[lead] < 0 else 0

        def load(where):
            value = gathered[index, where, :]
            return jnp.where(there, value[:, side : side + 64], 0.0)

        px, py = {-1: 0, 1: 9}.get(a), {-1: 0, 1: 9}.get(b)
        row = {-1: 7, 1: 16}.get(c)
        y_at, z_at = (7 if b < 0 else 0), (7 if c < 0 else 0)
        if lead == 0:
            if b == 0 and c == 0:
                face = load(pl.ds(0, 64))
                for y in range(8):
                    padded[pl.ds(at(px, 1 + y) + 8, 8), :] = face[8 * y : 8 * y + 8]
            elif c == 0:
                padded[pl.ds(at(px, py) + 8, 8), :] = load(pl.ds(8 * y_at, 8))
            elif b == 0:
                padded[pl.ds(at(px, 1) + row, 8, stride=ROWS), :] = load(pl.ds(z_at, 8, stride=8))
            else:
                padded[pl.ds(at(px, py) + row, 1), :] = load(pl.ds(8 * y_at + z_at, 1))
        elif lead == 1:
            if c == 0:
                face = load(pl.ds(64, 64))
                for x in range(8):
                    padded[pl.ds(at(1 + x, py) + 8, 8), :] = face[8 * x : 8 * x + 8]
            else:
                padded[pl.ds(at(1, py) + row, 8, stride=10 * ROWS), :] = load(pl.ds(64 + z_at, 8, stride=8))
        else:
            face = load(pl.ds(128, 64))
            for x in range(8):
                padded[pl.ds(at(1 + x, 1) + row, 8, stride=ROWS), :] = face[8 * x : 8 * x + 8]


def conv_kernel(place, neighbours, rows, *rest):
    blocks = rest[:16]
    high, low = rest[16:18]
    outs = rest[18:26]
    gathered, padded, columns, total, turned = rest[26:]
    for number in range(16):
        gathered[2 * number] = blocks[number][0]
        gathered[2 * number + 1] = blocks[number][1]
    for x in range(8):
        for y in range(8):
            padded[pl.ds(((1 + x) * 10 + 1 + y) * ROWS + 8, 8), :] = rows[pl.ds(x * 64 + y * 8, 8), :]
    fill_rims(place, neighbours, gathered, padded)
    for spot in range(100):
        before = padded[pl.ds(spot * ROWS + 7, 8), :]
        same = padded[pl.ds(spot * ROWS + 8, 8), :]
        after = padded[pl.ds(spot * ROWS + 9, 8), :]
        columns[spot // 10, spot % 10, :, 0:128] = jnp.concatenate([before, same], axis=1)
        columns[spot // 10, spot % 10, :, 128:192] = after

    for half in range(2):
        outputs = slice(256 * half, 256 * half + 256)
        for p in range(3):
            sums = None
            for q in range(3):
                values = columns[p : p + 8, q : q + 8, :, 0:192].reshape(512, 192)
                top = values.astype(BF16)
                rest_of = (values - top.astype(F32)).astype(BF16)
                tap = 9 * p + 3 * q
                heavy = high[tap : tap + 3, :, outputs].reshape(192, 256)
                light = low[tap : tap + 3, :, outputs].reshape(192, 256)
                dot = functools.partial(jnp.dot, preferred_element_type=F32)
                part = dot(top, heavy) + (dot(rest_of, heavy) + dot(top, light))
                sums = part if sums is None else sums + part
            if p == 0:
                total[...] = sums
            else:
                total[...] += sums
        turned[outputs, :] = total[...].T
    chip = place[3]
    for step in range(8):
        outs[step][...] = turned[pl.ds(pl.multiple_of((chip ^ step) * 64, 64), 64), :]


def conv(place, neighbours, rows, blocks, high, low):
    outs = tuple(arr((64, 512)) for _ in range(8))
    scratch = [
        pltpu.VMEM((32, 192, 128), F32),
        pltpu.VMEM((100 * ROWS, 64), F32),
        pltpu.VMEM((10, 10, 8, 256), F32),
        pltpu.VMEM((512, 256), F32),
        pltpu.VMEM((512, 512), F32),
    ]
    return call(conv_kernel, outs, scratch, flops=2 * 3 * 1024 * 1728 * 256, touched=8000000)(
        in_specs=[SMEM, SMEM] + [VMEM] * 19, out_specs=tuple([VMEM] * 8)
    )(place, neighbours, rows, *blocks, high, low)


def to_other_core(value):
    return lax.ppermute(value, "chan", [(i, i ^ 1) for i in range(16)])


def gather_faces(faces, weights):
    beside = lax.ppermute(faces, "leaf", [(i, i ^ 1) for i in range(16)])
    start = jnp.stack([faces, beside])
    found = [start] + [None] * 7
    up = down = start
    for step in range(1, 5):
        if step == 3:
            up, weights = lax.optimization_barrier((up, weights))
        up = lax.ppermute(up, "leaf", [(i, (i + 2) % 16) for i in range(16)])
        found[step] = up
        if step < 4:
            down = lax.ppermute(down, "leaf", [(i, (i - 2) % 16) for i in range(16)])
            found[8 - step] = down
    return found + [to_other_core(block) for block in found], weights


def add_over_chips(parts):
    landed = [parts[0]]
    for step in range(1, 8):
        landed.append(lax.ppermute(parts[step], "chan", [(i, i ^ (2 * step)) for i in range(16)]))
    return landed


def body(features, leaf_counts, occupancy, neighbours, weight_in, bias_in, weight_out, bias_out):
    leaf, chan = lax.axis_index("leaf"), lax.axis_index("chan")
    core = chan % 2
    place = jnp.stack([core, leaf % 2, leaf // 2, chan // 2]).astype(jnp.int32)
    others = to_other_core(lax.dynamic_index_in_dim(features, 1 - core, 1, keepdims=False))
    rows, faces = call(features_kernel, (arr((512, 64)), arr((192, 128))))(
        in_specs=[SMEM, SMEM, VMEM, VMEM, VMEM], out_specs=(VMEM, VMEM)
    )(place, leaf_counts, occupancy, features, others)
    biases = jnp.stack([bias_in, bias_out]).reshape(2, 32, 1)
    other_biases = to_other_core(jnp.stack([bias_in, bias_out])).reshape(2, 32, 1)
    weights = split_weights(place, weight_in, to_other_core(weight_in))
    weights_out = split_weights(place, weight_out, to_other_core(weight_out))

    blocks, weights = gather_faces(faces, weights)
    parts = add_over_chips(conv(place, neighbours, rows, blocks, *weights))
    rows, faces = call(hidden_kernel, (arr((512, 64)), arr((192, 128))))(
        in_specs=[SMEM, SMEM] + [VMEM] * 11, out_specs=(VMEM, VMEM)
    )(place, leaf_counts, occupancy, biases[0], other_biases[0], *parts)

    blocks, weights_out = gather_faces(faces, weights_out)
    parts = add_over_chips(conv(place, neighbours, rows, blocks, *weights_out))
    keep, give = call(result_kernel, (arr((32, 512)), arr((32, 512))))(
        in_specs=[SMEM, SMEM] + [VMEM] * 11, out_specs=(VMEM, VMEM)
    )(place, leaf_counts, occupancy, biases[1], other_biases[1], *parts)
    return call(merge_kernel, arr((32, 2, 512)))(in_specs=[SMEM, VMEM, VMEM], out_specs=VMEM)(
        place, keep, to_other_core(give)
    )


def solution(mesh):
    placed = (
        P("chan", "leaf", None),
        P("leaf"),
        P("leaf", None),
        P("leaf", None),
        P(None, "chan", None),
        P("chan"),
        P(None, "chan", None),
        P("chan"),
    )
    return jax.shard_map(
        body, mesh=mesh, in_specs=placed, out_specs=P("chan", "leaf", None), check_vma=False
    )
```

```python
import functools

import jax
import jax.numpy as jnp
from jax import lax
from jax.experimental import pallas as pl
from jax.experimental.pallas import tpu as pltpu
from jax.sharding import PartitionSpec as P

DIRECTIONS = [
    (first, second, third)
    for first in (-1, 0, 1)
    for second in (-1, 0, 1)
    for third in (-1, 0, 1)
    if (first, second, third) != (0, 0, 0)
]
VMEM = pl.BlockSpec(memory_space=pltpu.VMEM)
SMEM = pl.BlockSpec(memory_space=pltpu.SMEM)
F32 = jnp.float32
BF16 = jnp.bfloat16
ROWS = 24


def call(kernel, outs, scratch=(), flops=1000000, touched=1000000, room=16):
    return functools.partial(
        pl.pallas_call,
        kernel,
        out_shape=outs,
        scratch_shapes=list(scratch),
        compiler_params=pltpu.CompilerParams(vmem_limit_bytes=room * 1024 * 1024),
        cost_estimate=pl.CostEstimate(flops=flops, bytes_accessed=touched, transcendentals=0),
    )


def arr(shape, dtype=F32):
    return jax.ShapeDtypeStruct(shape, dtype)


def close(shape, dtype=F32):
    return pltpu.VMEM(shape, dtype)


def near(values):
    return [pltpu.with_memory_space_constraint(value, pltpu.VMEM) for value in values]


def weights_kernel(place, own, other, high, low):
    core = place[0]

    def step(tap, carry):
        mine, theirs = own[tap], other[tap]
        first = jnp.where(core == 0, mine, theirs)
        second = jnp.where(core == 0, theirs, mine)
        both = jnp.concatenate([first, second], axis=0)
        top = both.astype(BF16)
        high[tap] = top
        low[tap] = (both - top.astype(F32)).astype(BF16)
        return carry

    lax.fori_loop(0, 27, step, 0)


def split_weights(place, own, other):
    outs = (close((27, 64, 512), BF16), close((27, 64, 512), BF16))
    return call(weights_kernel, outs, flops=8000000, touched=9000000)(
        in_specs=[SMEM, VMEM, VMEM], out_specs=(VMEM, VMEM)
    )(place, own, other)


def cut_faces(rows, faces):
    faces[0:64, :] = jnp.concatenate([rows[0:64, :], rows[448:512, :]], axis=1)
    for x in range(8):
        faces[64 + 8 * x : 72 + 8 * x, :] = jnp.concatenate(
            [rows[64 * x : 64 * x + 8, :], rows[64 * x + 56 : 64 * x + 64, :]], axis=1
        )
    faces[128:192, :] = jnp.concatenate(
        [rows[pl.ds(0, 64, stride=8), :], rows[pl.ds(7, 64, stride=8), :]], axis=1
    )


def in_order(core, own, other):
    first = jnp.where(core == 0, own, other)
    second = jnp.where(core == 0, other, own)
    return jnp.concatenate([first, second], axis=0)


def active_voxels(core, counts, occupancy):
    chosen = jnp.where(core == 0, occupancy[0:1, :], occupancy[1:2, :]).astype(F32)
    return chosen * jnp.where(core < counts[0], 1.0, 0.0)


def features_kernel(place, counts, occupancy, own, other, rows, faces):
    core = place[0]
    mine = jnp.where(core == 0, own[:, 0, :], own[:, 1, :])
    theirs = jnp.where(core == 0, other[:, 0, :], other[:, 1, :])
    both = in_order(core, mine, theirs)
    rows[...] = (both * active_voxels(core, counts, occupancy)).T
    cut_faces(rows, faces)


def added(parts):
    value = parts[0][...]
    for part in parts[1:]:
        value = value + part[...]
    return value


def bias_row(core, number, own_bias, other_bias):
    own, other = own_bias[number : number + 1, :], other_bias[number : number + 1, :]
    first = jnp.where(core == 0, own, other)
    second = jnp.where(core == 0, other, own)
    return jnp.concatenate([first, second], axis=1)


def bias_column(row):
    wide = jnp.concatenate([row, row], axis=1)
    return jnp.broadcast_to(wide, (128, 128)).T[0:64, 0:1]


def hidden_kernel(place, counts, occupancy, own_bias, other_bias, *rest):
    core = place[0]
    rows, faces = rest[8:]
    bias = bias_column(bias_row(core, 0, own_bias, other_bias))
    value = jnp.maximum(added(rest[:8]) + bias, 0.0)
    rows[...] = (value * active_voxels(core, counts, occupancy)).T
    cut_faces(rows, faces)


def result_kernel(place, counts, occupancy, own_bias, other_bias, *rest):
    core = place[0]
    keep, give = rest[8:]
    bias = bias_column(bias_row(core, 1, own_bias, other_bias))
    value = (added(rest[:8]) + bias) * active_voxels(core, counts, occupancy)
    keep[...] = jnp.where(core == 0, value[0:32], value[32:64])
    give[...] = jnp.where(core == 0, value[32:64], value[0:32])


def merge_kernel(place, keep, got, out):
    core = place[0]
    out[:, 0, :] = jnp.where(core == 0, keep[...], got[...])
    out[:, 1, :] = jnp.where(core == 0, got[...], keep[...])


def fill_rims(place, neighbours, gathered, padded):
    core, low_x, depth = place[0], place[1], place[2]

    def at(x, y):
        return (x * 10 + y) * ROWS

    for number, (a, b, c) in enumerate(DIRECTIONS):
        entry = neighbours[place[0], number]
        there = entry >= 0
        found = jnp.clip(entry, 0, 31)
        index = (
            ((found & 1) ^ core) * 16
            + ((depth - (found >> 2)) & 7) * 2
            + (((found >> 1) & 1) ^ low_x)
        )

        lead = 0 if a else (1 if b else 2)
        side = 64 if (a, b, c)[lead] < 0 else 0

        def load(where):
            value = gathered[index, where, :]
            return jnp.where(there, value[:, side : side + 64], 0.0)

        px, py = {-1: 0, 1: 9}.get(a), {-1: 0, 1: 9}.get(b)
        row = {-1: 7, 1: 16}.get(c)
        y_at, z_at = (7 if b < 0 else 0), (7 if c < 0 else 0)
        if lead == 0:
            if b == 0 and c == 0:
                face = load(pl.ds(0, 64))
                for y in range(8):
                    padded[pl.ds(at(px, 1 + y) + 8, 8), :] = face[8 * y : 8 * y + 8]
            elif c == 0:
                padded[pl.ds(at(px, py) + 8, 8), :] = load(pl.ds(8 * y_at, 8))
            elif b == 0:
                padded[pl.ds(at(px, 1) + row, 8, stride=ROWS), :] = load(pl.ds(z_at, 8, stride=8))
            else:
                padded[pl.ds(at(px, py) + row, 1), :] = load(pl.ds(8 * y_at + z_at, 1))
        elif lead == 1:
            if c == 0:
                face = load(pl.ds(64, 64))
                for x in range(8):
                    padded[pl.ds(at(1 + x, py) + 8, 8), :] = face[8 * x : 8 * x + 8]
            else:
                padded[pl.ds(at(1, py) + row, 8, stride=10 * ROWS), :] = load(pl.ds(64 + z_at, 8, stride=8))
        else:
            face = load(pl.ds(128, 64))
            for x in range(8):
                padded[pl.ds(at(1 + x, 1) + row, 8, stride=ROWS), :] = face[8 * x : 8 * x + 8]


def conv_kernel(place, neighbours, rows, *rest):
    blocks = rest[:16]
    high, low = rest[16:18]
    outs = rest[18:26]
    gathered, padded, columns, total, turned = rest[26:]
    for number in range(16):
        gathered[2 * number] = blocks[number][0]
        gathered[2 * number + 1] = blocks[number][1]
    for x in range(8):
        for y in range(8):
            padded[pl.ds(((1 + x) * 10 + 1 + y) * ROWS + 8, 8), :] = rows[pl.ds(x * 64 + y * 8, 8), :]
    fill_rims(place, neighbours, gathered, padded)
    for spot in range(100):
        before = padded[pl.ds(spot * ROWS + 7, 8), :]
        same = padded[pl.ds(spot * ROWS + 8, 8), :]
        after = padded[pl.ds(spot * ROWS + 9, 8), :]
        columns[spot // 10, spot % 10, :, 0:128] = jnp.concatenate([before, same], axis=1)
        columns[spot // 10, spot % 10, :, 128:192] = after

    dot = functools.partial(jnp.dot, preferred_element_type=F32)
    for p in range(3):
        sums = None
        for q in range(3):
            values = columns[p : p + 8, q : q + 8, :, 0:192].reshape(512, 192)
            top = values.astype(BF16)
            rest_of = (values - top.astype(F32)).astype(BF16)
            tap = 9 * p + 3 * q
            heavy = high[tap : tap + 3].reshape(192, 512)
            light = low[tap : tap + 3].reshape(192, 512)
            part = dot(top, heavy) + (dot(rest_of, heavy) + dot(top, light))
            sums = part if sums is None else sums + part
        if p == 0:
            total[...] = sums
        else:
            total[...] += sums
    turned[...] = total[...].T
    chip = place[3]
    for step, (along, across) in enumerate(ROUTES + ((0, 0),)):
        target = (((chip >> 1) + along) & 3) * 2 + ((chip & 1) ^ across)
        outs[step][...] = turned[pl.ds(pl.multiple_of(target * 64, 64), 64), :]


def conv(place, neighbours, rows, blocks, high, low):
    outs = tuple(close((64, 512)) for _ in range(8))
    scratch = [
        pltpu.VMEM((32, 192, 128), F32),
        pltpu.VMEM((100 * ROWS, 64), F32),
        pltpu.VMEM((10, 10, 8, 256), F32),
        pltpu.VMEM((512, 512), F32),
        pltpu.VMEM((512, 512), F32),
    ]
    return call(
        conv_kernel, outs, scratch, flops=2 * 3 * 1024 * 1728 * 256, touched=8000000, room=24
    )(
        in_specs=[SMEM, SMEM] + [VMEM] * 19, out_specs=tuple([VMEM] * 8)
    )(place, neighbours, *near([rows, *blocks, high, low]))


def to_other_core(value):
    return lax.ppermute(value, "chan", [(i, i ^ 1) for i in range(16)])


def gather_faces(faces, weights):
    beside = lax.ppermute(faces, "leaf", [(i, i ^ 1) for i in range(16)])
    start = jnp.stack([faces, beside])
    found = [start] + [None] * 7
    up = down = start
    for step in range(1, 5):
        if step == 3:
            up, weights = lax.optimization_barrier((up, weights))
        up = lax.ppermute(up, "leaf", [(i, (i + 2) % 16) for i in range(16)])
        found[step] = up
        if step < 4:
            down = lax.ppermute(down, "leaf", [(i, (i - 2) % 16) for i in range(16)])
            found[8 - step] = down
    return found + [to_other_core(block) for block in found], weights


ROUTES = ((2, 1), (1, 1), (3, 1), (2, 0), (0, 1), (1, 0), (3, 0))


def route_target(device, route):
    return (device // 4 + route[0]) % 4 * 4 + ((device % 4) ^ (2 * route[1]))


def add_over_chips(parts):
    landed = [parts[7]]
    for part, route in zip(parts, ROUTES):
        landed.append(lax.ppermute(part, "chan", [(i, route_target(i, route)) for i in range(16)]))
    return landed


def body(features, leaf_counts, occupancy, neighbours, weight_in, bias_in, weight_out, bias_out):
    leaf, chan = lax.axis_index("leaf"), lax.axis_index("chan")
    core = chan % 2
    place = jnp.stack([core, leaf % 2, leaf // 2, chan // 2]).astype(jnp.int32)
    others = to_other_core(features)
    rows, faces = call(features_kernel, (close((512, 64)), close((192, 128))))(
        in_specs=[SMEM, SMEM, VMEM, VMEM, VMEM], out_specs=(VMEM, VMEM)
    )(place, leaf_counts, occupancy, features, *near([others]))
    biases = jnp.stack([bias_in, bias_out])
    other_biases = to_other_core(biases)
    weights = split_weights(place, weight_in, to_other_core(weight_in))
    weights_out = split_weights(place, weight_out, to_other_core(weight_out))

    blocks, weights = gather_faces(faces, weights)
    parts = add_over_chips(conv(place, neighbours, rows, blocks, *weights))
    rows, faces = call(hidden_kernel, (close((512, 64)), close((192, 128))))(
        in_specs=[SMEM, SMEM] + [VMEM] * 11, out_specs=(VMEM, VMEM)
    )(place, leaf_counts, occupancy, biases, other_biases, *near(parts))

    blocks, weights_out = gather_faces(faces, weights_out)
    parts = add_over_chips(conv(place, neighbours, rows, blocks, *weights_out))
    keep, give = call(result_kernel, (close((32, 512)), close((32, 512))))(
        in_specs=[SMEM, SMEM] + [VMEM] * 11, out_specs=(VMEM, VMEM)
    )(place, leaf_counts, occupancy, biases, other_biases, *near(parts))
    return call(merge_kernel, arr((32, 2, 512)))(in_specs=[SMEM, VMEM, VMEM], out_specs=VMEM)(
        place, *near([keep, to_other_core(give)])
    )


def solution(mesh):
    placed = (
        P("chan", "leaf", None),
        P("leaf"),
        P("leaf", None),
        P("leaf", None),
        P(None, "chan", None),
        P("chan"),
        P(None, "chan", None),
        P("chan"),
    )
    return jax.shard_map(
        body, mesh=mesh, in_specs=placed, out_specs=P("chan", "leaf", None), check_vma=False
    )
```

```python
import functools

import jax
import jax.numpy as jnp
from jax import lax
from jax.experimental import pallas as pl
from jax.experimental.pallas import tpu as pltpu
from jax.sharding import PartitionSpec as P

DIRECTIONS = [
    (first, second, third)
    for first in (-1, 0, 1)
    for second in (-1, 0, 1)
    for third in (-1, 0, 1)
    if (first, second, third) != (0, 0, 0)
]
VMEM = pl.BlockSpec(memory_space=pltpu.VMEM)
SMEM = pl.BlockSpec(memory_space=pltpu.SMEM)
F32 = jnp.float32
BF16 = jnp.bfloat16
ROWS = 24


def call(kernel, outs, scratch=(), flops=1000000, touched=1000000, room=16):
    return functools.partial(
        pl.pallas_call,
        kernel,
        out_shape=outs,
        scratch_shapes=list(scratch),
        compiler_params=pltpu.CompilerParams(vmem_limit_bytes=room * 1024 * 1024),
        cost_estimate=pl.CostEstimate(flops=flops, bytes_accessed=touched, transcendentals=0),
    )


def arr(shape, dtype=F32):
    return jax.ShapeDtypeStruct(shape, dtype)


def close(shape, dtype=F32):
    return pltpu.VMEM(shape, dtype)


def near(values):
    return [pltpu.with_memory_space_constraint(value, pltpu.VMEM) for value in values]


def weights_kernel(place, own, other, high, low):
    core = place[0]

    def step(tap, carry):
        mine, theirs = own[tap], other[tap]
        first = jnp.where(core == 0, mine, theirs)
        second = jnp.where(core == 0, theirs, mine)
        both = jnp.concatenate([first, second], axis=0)
        top = both.astype(BF16)
        high[tap] = top
        low[tap] = (both - top.astype(F32)).astype(BF16)
        return carry

    lax.fori_loop(0, 27, step, 0)


def split_weights(place, own, other):
    outs = (close((27, 64, 512), BF16), close((27, 64, 512), BF16))
    return call(weights_kernel, outs, flops=8000000, touched=9000000)(
        in_specs=[SMEM, VMEM, VMEM], out_specs=(VMEM, VMEM)
    )(place, own, other)


def cut_faces(rows, faces):
    faces[0:64, :] = jnp.concatenate([rows[0:64, :], rows[448:512, :]], axis=1)
    for x in range(8):
        faces[64 + 8 * x : 72 + 8 * x, :] = jnp.concatenate(
            [rows[64 * x : 64 * x + 8, :], rows[64 * x + 56 : 64 * x + 64, :]], axis=1
        )
    faces[128:192, :] = jnp.concatenate(
        [rows[pl.ds(0, 64, stride=8), :], rows[pl.ds(7, 64, stride=8), :]], axis=1
    )


def in_order(core, own, other):
    first = jnp.where(core == 0, own, other)
    second = jnp.where(core == 0, other, own)
    return jnp.concatenate([first, second], axis=0)


def active_voxels(core, counts, occupancy):
    chosen = jnp.where(core == 0, occupancy[0:1, :], occupancy[1:2, :]).astype(F32)
    return chosen * jnp.where(core < counts[0], 1.0, 0.0)


def features_kernel(place, counts, occupancy, own, other, rows, faces):
    core = place[0]
    mine = jnp.where(core == 0, own[:, 0, :], own[:, 1, :])
    theirs = jnp.where(core == 0, other[:, 0, :], other[:, 1, :])
    both = in_order(core, mine, theirs)
    rows[...] = (both * active_voxels(core, counts, occupancy)).T
    cut_faces(rows, faces)


def added(parts):
    value = parts[0][...]
    for part in parts[1:]:
        value = value + part[...]
    return value


def bias_row(core, number, own_bias, other_bias):
    own, other = own_bias[number : number + 1, :], other_bias[number : number + 1, :]
    first = jnp.where(core == 0, own, other)
    second = jnp.where(core == 0, other, own)
    return jnp.concatenate([first, second], axis=1)


def bias_column(row):
    wide = jnp.concatenate([row, row], axis=1)
    return jnp.broadcast_to(wide, (128, 128)).T[0:64, 0:1]


def hidden_kernel(place, counts, occupancy, own_bias, other_bias, *rest):
    core = place[0]
    rows, faces = rest[8:]
    bias = bias_column(bias_row(core, 0, own_bias, other_bias))
    value = jnp.maximum(added(rest[:8]) + bias, 0.0)
    rows[...] = (value * active_voxels(core, counts, occupancy)).T
    cut_faces(rows, faces)


def result_kernel(place, counts, occupancy, own_bias, other_bias, *rest):
    core = place[0]
    keep, give = rest[8:]
    bias = bias_column(bias_row(core, 1, own_bias, other_bias))
    value = (added(rest[:8]) + bias) * active_voxels(core, counts, occupancy)
    keep[...] = jnp.where(core == 0, value[0:32], value[32:64])
    give[...] = jnp.where(core == 0, value[32:64], value[0:32])


def merge_kernel(place, keep, got, out):
    core = place[0]
    out[:, 0, :] = jnp.where(core == 0, keep[...], got[...])
    out[:, 1, :] = jnp.where(core == 0, got[...], keep[...])


def rim_list():
    listed, begin = [], 192
    corner = 240
    for a, b, c in DIRECTIONS:
        steps = [step for step in (a, b, c) if step]
        if steps[0] < 0:
            continue
        if len(steps) == 1:
            listed.append(((a, b, c), 64 * (0 if a else (1 if b else 2)), 64))
        elif len(steps) == 2:
            listed.append(((a, b, c), begin, 8))
            begin += 8
        else:
            listed.append(((a, b, c), corner, 1))
            corner += 1
    return listed


RIM_ROWS = 248


def face_rows(offsets):
    a, b, c = offsets
    y_at, z_at = (7 if b < 0 else 0), (7 if c < 0 else 0)
    if a:
        if b == 0:
            return pl.ds(0, 64) if c == 0 else pl.ds(z_at, 8, stride=8)
        return pl.ds(8 * y_at, 8) if c == 0 else pl.ds(8 * y_at + z_at, 1)
    if b:
        return pl.ds(64, 64) if c == 0 else pl.ds(64 + z_at, 8, stride=8)
    return pl.ds(128, 64)


def rims_kernel(place, own_table, other_table, *rest):
    blocks, outs, gathered = rest[:8], rest[8:12], rest[12]
    core, low_x, depth = place[0], place[1], place[2]
    for number in range(8):
        gathered[number] = blocks[number][...]
    for peer in range(4):
        table = other_table if peer & 1 else own_table
        slot = core ^ (peer >> 1)
        out = outs[peer]
        out[240:248, :] = jnp.zeros((8, 128), F32)

        def load(offsets):
            entry = table[slot, DIRECTIONS.index(offsets)]
            found = jnp.clip(entry, 0, 31)
            here = (entry >= 0) & ((found & 1) == core) & (((found >> 1) & 1) == low_x)
            value = gathered[(depth - (found >> 2)) & 7, face_rows(offsets), :]
            return jnp.where(here, value, 0.0)

        for offsets, begin, count in rim_list():
            up, down = load(offsets), load(tuple(-step for step in offsets))
            lane = lax.broadcasted_iota(jnp.int32, (count, 128), 1)
            out[begin : begin + count, :] = jnp.where(lane < 64, up, down)


def cut_rims(place, own_table, other_table, blocks):
    outs = tuple(close((RIM_ROWS, 128)) for _ in range(4))
    return call(rims_kernel, outs, [pltpu.VMEM((8, 192, 128), F32)], touched=1000000)(
        in_specs=[SMEM, SMEM, SMEM] + [VMEM] * 8, out_specs=tuple([VMEM] * 4)
    )(place, own_table, other_table, *near(blocks))


def fill_rims(rims, padded):
    def at(x, y):
        return (x * 10 + y) * ROWS

    for upward, begin, count in rim_list():
        for sign in (1, -1):
            a, b, c = (sign * step for step in upward)
            side = 0 if sign > 0 else 64
            value = rims[begin : begin + count, side : side + 64]
            px, py = {-1: 0, 1: 9}.get(a), {-1: 0, 1: 9}.get(b)
            row = {-1: 7, 0: 8, 1: 16}[c]
            if count == 64:
                for n in range(8):
                    piece = value[8 * n : 8 * n + 8]
                    if a:
                        padded[pl.ds(at(px, 1 + n) + 8, 8), :] = piece
                    elif b:
                        padded[pl.ds(at(1 + n, py) + 8, 8), :] = piece
                    else:
                        padded[pl.ds(at(1 + n, 1) + row, 8, stride=ROWS), :] = piece
            elif count == 1:
                padded[pl.ds(at(px, py) + row, 1), :] = value
            elif c == 0:
                padded[pl.ds(at(px, py) + 8, 8), :] = value
            elif a:
                padded[pl.ds(at(px, 1) + row, 8, stride=ROWS), :] = value
            else:
                padded[pl.ds(at(1, py) + row, 8, stride=10 * ROWS), :] = value


def conv_kernel(place, rows, *rest):
    pieces = rest[:4]
    high, low = rest[4:6]
    outs = rest[6:14]
    rims, padded, columns, total, turned = rest[14:]
    rims[...] = (pieces[0][...] + pieces[1][...]) + (pieces[2][...] + pieces[3][...])
    for x in range(8):
        for y in range(8):
            padded[pl.ds(((1 + x) * 10 + 1 + y) * ROWS + 8, 8), :] = rows[pl.ds(x * 64 + y * 8, 8), :]
    fill_rims(rims, padded)
    for spot in range(100):
        before = padded[pl.ds(spot * ROWS + 7, 8), :]
        same = padded[pl.ds(spot * ROWS + 8, 8), :]
        after = padded[pl.ds(spot * ROWS + 9, 8), :]
        columns[spot // 10, spot % 10, :, 0:128] = jnp.concatenate([before, same], axis=1)
        columns[spot // 10, spot % 10, :, 128:192] = after

    dot = functools.partial(jnp.dot, preferred_element_type=F32)
    for p in range(3):
        sums = None
        for q in range(3):
            values = columns[p : p + 8, q : q + 8, :, 0:192].reshape(512, 192)
            top = values.astype(BF16)
            rest_of = (values - top.astype(F32)).astype(BF16)
            tap = 9 * p + 3 * q
            heavy = high[tap : tap + 3].reshape(192, 512)
            light = low[tap : tap + 3].reshape(192, 512)
            part = dot(top, heavy) + (dot(rest_of, heavy) + dot(top, light))
            sums = part if sums is None else sums + part
        if p == 0:
            total[...] = sums
        else:
            total[...] += sums
    turned[...] = total[...].T
    chip = place[3]
    for step, (along, across) in enumerate(ROUTES + ((0, 0),)):
        target = (((chip >> 1) + along) & 3) * 2 + ((chip & 1) ^ across)
        outs[step][...] = turned[pl.ds(pl.multiple_of(target * 64, 64), 64), :]


def conv(place, rows, rims, high, low):
    outs = tuple(close((64, 512)) for _ in range(8))
    scratch = [
        pltpu.VMEM((RIM_ROWS, 128), F32),
        pltpu.VMEM((100 * ROWS, 64), F32),
        pltpu.VMEM((10, 10, 8, 256), F32),
        pltpu.VMEM((512, 512), F32),
        pltpu.VMEM((512, 512), F32),
    ]
    return call(
        conv_kernel, outs, scratch, flops=2 * 3 * 1024 * 1728 * 256, touched=8000000, room=24
    )(
        in_specs=[SMEM] + [VMEM] * 7, out_specs=tuple([VMEM] * 8)
    )(place, *near([rows, *rims, high, low]))


def to_other_core(value):
    return lax.ppermute(value, "chan", [(i, i ^ 1) for i in range(16)])


def to_other_x(value):
    return lax.ppermute(value, "leaf", [(i, i ^ 1) for i in range(16)])


def to_other_both(value):
    pairs = [(16 * i + j, 16 * (i ^ 1) + (j ^ 1)) for i in range(16) for j in range(16)]
    return lax.ppermute(value, ("leaf", "chan"), pairs)


def gather_rims(place, tables, faces, early=(), late=()):
    found = [faces] + [None] * 7
    for step in (4, 3, -3, 2, -2, 1, -1):
        if step == 1 and early:
            faces, early, found[4] = lax.optimization_barrier((faces, early, found[4]))
        found[step % 8] = lax.ppermute(faces, "leaf", [(i, (i + 2 * step) % 16) for i in range(16)])
    found, late = lax.optimization_barrier((found, late))
    tables = early[0] if early else tables
    own, beside, across, both = cut_rims(place, *tables, found)
    return [own, to_other_both(both), to_other_x(beside), to_other_core(across)], early, late


ROUTES = ((2, 1), (1, 1), (3, 1), (2, 0), (0, 1), (1, 0), (3, 0))


def route_target(device, route):
    return (device // 4 + route[0]) % 4 * 4 + ((device % 4) ^ (2 * route[1]))


def add_over_chips(parts):
    landed = [parts[7]]
    for part, route in zip(parts, ROUTES):
        landed.append(lax.ppermute(part, "chan", [(i, route_target(i, route)) for i in range(16)]))
    return landed


def body(features, leaf_counts, occupancy, neighbours, weight_in, bias_in, weight_out, bias_out):
    leaf, chan = lax.axis_index("leaf"), lax.axis_index("chan")
    core = chan % 2
    place = jnp.stack([core, leaf % 2, leaf // 2, chan // 2]).astype(jnp.int32)
    others = to_other_core(features)
    _, weight_in, weight_out = lax.optimization_barrier((others, weight_in, weight_out))
    rows, faces = call(features_kernel, (close((512, 64)), close((192, 128))))(
        in_specs=[SMEM, SMEM, VMEM, VMEM, VMEM], out_specs=(VMEM, VMEM)
    )(place, leaf_counts, occupancy, features, *near([others]))
    tables = neighbours, to_other_x(neighbours)
    biases = jnp.stack([bias_in, bias_out])
    biases = biases, to_other_core(biases)
    weights = split_weights(place, weight_in, to_other_core(weight_in))
    weights_out = split_weights(place, weight_out, to_other_core(weight_out))

    rims, (tables, biases), (weights, weights_out) = gather_rims(
        place, tables, faces, (tables, biases), (weights, weights_out)
    )
    parts = add_over_chips(conv(place, rows, rims, *weights))
    rows, faces = call(hidden_kernel, (close((512, 64)), close((192, 128))))(
        in_specs=[SMEM, SMEM] + [VMEM] * 11, out_specs=(VMEM, VMEM)
    )(place, leaf_counts, occupancy, *biases, *near(parts))

    rims, _, _ = gather_rims(place, tables, faces)
    parts = add_over_chips(conv(place, rows, rims, *weights_out))
    keep, give = call(result_kernel, (close((32, 512)), close((32, 512))))(
        in_specs=[SMEM, SMEM] + [VMEM] * 11, out_specs=(VMEM, VMEM)
    )(place, leaf_counts, occupancy, *biases, *near(parts))
    return call(merge_kernel, arr((32, 2, 512)))(in_specs=[SMEM, VMEM, VMEM], out_specs=VMEM)(
        place, *near([keep, to_other_core(give)])
    )


def solution(mesh):
    placed = (
        P("chan", "leaf", None),
        P("leaf"),
        P("leaf", None),
        P("leaf", None),
        P(None, "chan", None),
        P("chan"),
        P(None, "chan", None),
        P("chan"),
    )
    return jax.shard_map(
        body, mesh=mesh, in_specs=placed, out_specs=P("chan", "leaf", None), check_vma=False
    )
```

```python
import functools

import jax
import jax.numpy as jnp
from jax import lax
from jax.experimental import pallas as pl
from jax.experimental.pallas import tpu as pltpu
from jax.sharding import PartitionSpec as P

DIRECTIONS = [
    (first, second, third)
    for first in (-1, 0, 1)
    for second in (-1, 0, 1)
    for third in (-1, 0, 1)
    if (first, second, third) != (0, 0, 0)
]
VMEM = pl.BlockSpec(memory_space=pltpu.VMEM)
SMEM = pl.BlockSpec(memory_space=pltpu.SMEM)
F32 = jnp.float32
BF16 = jnp.bfloat16
ROWS = 24


def call(kernel, outs, scratch=(), flops=1000000, touched=1000000, room=16):
    return functools.partial(
        pl.pallas_call,
        kernel,
        out_shape=outs,
        scratch_shapes=list(scratch),
        compiler_params=pltpu.CompilerParams(vmem_limit_bytes=room * 1024 * 1024),
        cost_estimate=pl.CostEstimate(flops=flops, bytes_accessed=touched, transcendentals=0),
    )


def arr(shape, dtype=F32):
    return jax.ShapeDtypeStruct(shape, dtype)


def close(shape, dtype=F32):
    return pltpu.VMEM(shape, dtype)


def near(values):
    return [pltpu.with_memory_space_constraint(value, pltpu.VMEM) for value in values]


def weights_kernel(place, own, other, high, low):
    core = place[0]

    def step(tap, carry):
        mine, theirs = own[tap], other[tap]
        first = jnp.where(core == 0, mine, theirs)
        second = jnp.where(core == 0, theirs, mine)
        both = jnp.concatenate([first, second], axis=0)
        top = both.astype(BF16)
        high[tap] = top
        low[tap] = (both - top.astype(F32)).astype(BF16)
        return carry

    lax.fori_loop(0, 27, step, 0)


def split_weights(place, own, other):
    outs = (close((27, 64, 512), BF16), close((27, 64, 512), BF16))
    return call(weights_kernel, outs, flops=8000000, touched=9000000)(
        in_specs=[SMEM, VMEM, VMEM], out_specs=(VMEM, VMEM)
    )(place, own, other)


def cut_faces(rows, faces):
    faces[0:64, :] = jnp.concatenate([rows[0:64, :], rows[448:512, :]], axis=1)
    for x in range(8):
        faces[64 + 8 * x : 72 + 8 * x, :] = jnp.concatenate(
            [rows[64 * x : 64 * x + 8, :], rows[64 * x + 56 : 64 * x + 64, :]], axis=1
        )
    faces[128:192, :] = jnp.concatenate(
        [rows[pl.ds(0, 64, stride=8), :], rows[pl.ds(7, 64, stride=8), :]], axis=1
    )


def in_order(core, own, other):
    first = jnp.where(core == 0, own, other)
    second = jnp.where(core == 0, other, own)
    return jnp.concatenate([first, second], axis=0)


def active_voxels(core, counts, occupancy):
    chosen = jnp.where(core == 0, occupancy[0:1, :], occupancy[1:2, :]).astype(F32)
    return chosen * jnp.where(core < counts[0], 1.0, 0.0)


def features_kernel(place, counts, occupancy, own, other, rows, faces):
    core = place[0]
    mine = jnp.where(core == 0, own[:, 0, :], own[:, 1, :])
    theirs = jnp.where(core == 0, other[:, 0, :], other[:, 1, :])
    both = in_order(core, mine, theirs)
    rows[...] = (both * active_voxels(core, counts, occupancy)).T
    cut_faces(rows, faces)


def added(parts):
    value = parts[0][...]
    for part in parts[1:]:
        value = value + part[...]
    return value


def bias_row(core, number, own_bias, other_bias):
    own, other = own_bias[number : number + 1, :], other_bias[number : number + 1, :]
    first = jnp.where(core == 0, own, other)
    second = jnp.where(core == 0, other, own)
    return jnp.concatenate([first, second], axis=1)


def bias_column(row):
    wide = jnp.concatenate([row, row], axis=1)
    return jnp.broadcast_to(wide, (128, 128)).T[0:64, 0:1]


def hidden_kernel(place, counts, occupancy, own_bias, other_bias, *rest):
    core = place[0]
    rows, faces = rest[8:]
    bias = bias_column(bias_row(core, 0, own_bias, other_bias))
    value = jnp.maximum(added(rest[:8]) + bias, 0.0)
    rows[...] = (value * active_voxels(core, counts, occupancy)).T
    cut_faces(rows, faces)


def result_kernel(place, counts, occupancy, own_bias, other_bias, *rest):
    core = place[0]
    keep, give = rest[8:]
    bias = bias_column(bias_row(core, 1, own_bias, other_bias))
    value = (added(rest[:8]) + bias) * active_voxels(core, counts, occupancy)
    keep[...] = jnp.where(core == 0, value[0:32], value[32:64])
    give[...] = jnp.where(core == 0, value[32:64], value[0:32])


def merge_kernel(place, keep, got, out):
    core = place[0]
    out[:, 0, :] = jnp.where(core == 0, keep[...], got[...])
    out[:, 1, :] = jnp.where(core == 0, got[...], keep[...])


def rim_list():
    listed, begin = [], 192
    corner = 240
    for a, b, c in DIRECTIONS:
        steps = [step for step in (a, b, c) if step]
        if steps[0] < 0:
            continue
        if len(steps) == 1:
            listed.append(((a, b, c), 64 * (0 if a else (1 if b else 2)), 64))
        elif len(steps) == 2:
            listed.append(((a, b, c), begin, 8))
            begin += 8
        else:
            listed.append(((a, b, c), corner, 1))
            corner += 1
    return listed


RIM_ROWS = 248
SENT = (4, 3, -3, 2, -2, 1, -1)


def face_rows(offsets):
    a, b, c = offsets
    y_at, z_at = (7 if b < 0 else 0), (7 if c < 0 else 0)
    if a:
        if b == 0:
            return pl.ds(0, 64) if c == 0 else pl.ds(z_at, 8, stride=8)
        return pl.ds(8 * y_at, 8) if c == 0 else pl.ds(8 * y_at + z_at, 1)
    if b:
        return pl.ds(64, 64) if c == 0 else pl.ds(64 + z_at, 8, stride=8)
    return pl.ds(128, 64)


def rims_kernel(place, own_table, other_table, *rest):
    blocks, outs, gathered = rest[:8], rest[8:12], rest[12]
    core, low_x, depth = place[0], place[1], place[2]
    for number, step in enumerate(SENT + (0,)):
        gathered[step % 8] = blocks[number][...]
    for peer in range(4):
        table = other_table if peer & 1 else own_table
        slot = core ^ (peer >> 1)
        out = outs[peer]
        out[240:248, :] = jnp.zeros((8, 128), F32)

        def load(offsets):
            entry = table[slot, DIRECTIONS.index(offsets)]
            found = jnp.clip(entry, 0, 31)
            here = (entry >= 0) & ((found & 1) == core) & (((found >> 1) & 1) == low_x)
            value = gathered[(depth - (found >> 2)) & 7, face_rows(offsets), :]
            return jnp.where(here, value, 0.0)

        for offsets, begin, count in rim_list():
            up, down = load(offsets), load(tuple(-step for step in offsets))
            lane = lax.broadcasted_iota(jnp.int32, (count, 128), 1)
            out[begin : begin + count, :] = jnp.where(lane < 64, up, down)


def cut_rims(place, own_table, other_table, blocks):
    outs = tuple(close((RIM_ROWS, 128)) for _ in range(4))
    return call(rims_kernel, outs, [pltpu.VMEM((8, 192, 128), F32)], touched=1000000)(
        in_specs=[SMEM, SMEM, SMEM] + [VMEM] * 8, out_specs=tuple([VMEM] * 4)
    )(place, own_table, other_table, *near(blocks))


def fill_rims(rims, padded):
    def at(x, y):
        return (x * 10 + y) * ROWS

    for upward, begin, count in rim_list():
        for sign in (1, -1):
            a, b, c = (sign * step for step in upward)
            side = 0 if sign > 0 else 64
            value = rims[begin : begin + count, side : side + 64]
            px, py = {-1: 0, 1: 9}.get(a), {-1: 0, 1: 9}.get(b)
            row = {-1: 7, 0: 8, 1: 16}[c]
            if count == 64:
                for n in range(8):
                    piece = value[8 * n : 8 * n + 8]
                    if a:
                        padded[pl.ds(at(px, 1 + n) + 8, 8), :] = piece
                    elif b:
                        padded[pl.ds(at(1 + n, py) + 8, 8), :] = piece
                    else:
                        padded[pl.ds(at(1 + n, 1) + row, 8, stride=ROWS), :] = piece
            elif count == 1:
                padded[pl.ds(at(px, py) + row, 1), :] = value
            elif c == 0:
                padded[pl.ds(at(px, py) + 8, 8), :] = value
            elif a:
                padded[pl.ds(at(px, 1) + row, 8, stride=ROWS), :] = value
            else:
                padded[pl.ds(at(1, py) + row, 8, stride=10 * ROWS), :] = value


def conv_kernel(place, rows, *rest):
    pieces = rest[:4]
    high, low = rest[4:6]
    outs = rest[6:14]
    rims, padded, columns, total, turned = rest[14:]
    rims[...] = (pieces[0][...] + pieces[1][...]) + (pieces[2][...] + pieces[3][...])
    for x in range(8):
        for y in range(8):
            padded[pl.ds(((1 + x) * 10 + 1 + y) * ROWS + 8, 8), :] = rows[pl.ds(x * 64 + y * 8, 8), :]
    fill_rims(rims, padded)
    for spot in range(100):
        before = padded[pl.ds(spot * ROWS + 7, 8), :]
        same = padded[pl.ds(spot * ROWS + 8, 8), :]
        after = padded[pl.ds(spot * ROWS + 9, 8), :]
        columns[spot // 10, spot % 10, :, 0:128] = jnp.concatenate([before, same], axis=1)
        columns[spot // 10, spot % 10, :, 128:192] = after

    dot = functools.partial(jnp.dot, preferred_element_type=F32)
    for p in range(3):
        sums = None
        for q in range(3):
            values = columns[p : p + 8, q : q + 8, :, 0:192].reshape(512, 192)
            top = values.astype(BF16)
            rest_of = (values - top.astype(F32)).astype(BF16)
            tap = 9 * p + 3 * q
            heavy = high[tap : tap + 3].reshape(192, 512)
            light = low[tap : tap + 3].reshape(192, 512)
            part = dot(top, heavy) + (dot(rest_of, heavy) + dot(top, light))
            sums = part if sums is None else sums + part
        if p == 0:
            total[...] = sums
        else:
            total[...] += sums
    turned[...] = total[...].T
    chip = place[3]
    for step, (along, across) in enumerate(ROUTES + ((0, 0),)):
        target = (((chip >> 1) + along) & 3) * 2 + ((chip & 1) ^ across)
        outs[step][...] = turned[pl.ds(pl.multiple_of(target * 64, 64), 64), :]


def conv(place, rows, rims, high, low):
    outs = tuple(close((64, 512)) for _ in range(8))
    scratch = [
        pltpu.VMEM((RIM_ROWS, 128), F32),
        pltpu.VMEM((100 * ROWS, 64), F32),
        pltpu.VMEM((10, 10, 8, 256), F32),
        pltpu.VMEM((512, 512), F32),
        pltpu.VMEM((512, 512), F32),
    ]
    return call(
        conv_kernel, outs, scratch, flops=2 * 3 * 1024 * 1728 * 256, touched=8000000, room=24
    )(
        in_specs=[SMEM] + [VMEM] * 7, out_specs=tuple([VMEM] * 8)
    )(place, *near([rows, *rims, high, low]))


def to_other_core(value):
    return lax.ppermute(value, "chan", [(i, i ^ 1) for i in range(16)])


def to_other_x(value):
    return lax.ppermute(value, "leaf", [(i, i ^ 1) for i in range(16)])


def to_other_both(value):
    pairs = [(16 * i + j, 16 * (i ^ 1) + (j ^ 1)) for i in range(16) for j in range(16)]
    return lax.ppermute(value, ("leaf", "chan"), pairs)


def gather_rims(place, tables, faces, early=(), weight=None):
    found = []
    for step in SENT:
        if step == 1 and early:
            faces, early, found[0] = lax.optimization_barrier((faces, early, found[0]))
        found.append(lax.ppermute(faces, "leaf", [(i, (i + 2 * step) % 16) for i in range(16)]))
    if weight is not None:
        found[1], weight = lax.optimization_barrier((found[1], weight))
        weight = split_weights(place, weight, to_other_core(weight))
        found, weight = lax.optimization_barrier((found, weight))
    tables = early[0] if early else tables
    own, beside, across, both = cut_rims(place, *tables, found + [faces])
    return [own, to_other_both(both), to_other_x(beside), to_other_core(across)], early, weight


ROUTES = ((2, 1), (1, 1), (3, 1), (2, 0), (0, 1), (1, 0), (3, 0))


def route_target(device, route):
    return (device // 4 + route[0]) % 4 * 4 + ((device % 4) ^ (2 * route[1]))


def add_over_chips(parts):
    landed = [parts[7]]
    for part, route in zip(parts, ROUTES):
        landed.append(lax.ppermute(part, "chan", [(i, route_target(i, route)) for i in range(16)]))
    return landed


def body(features, leaf_counts, occupancy, neighbours, weight_in, bias_in, weight_out, bias_out):
    leaf, chan = lax.axis_index("leaf"), lax.axis_index("chan")
    core = chan % 2
    place = jnp.stack([core, leaf % 2, leaf // 2, chan // 2]).astype(jnp.int32)
    others = to_other_core(features)
    rows, faces = call(features_kernel, (close((512, 64)), close((192, 128))))(
        in_specs=[SMEM, SMEM, VMEM, VMEM, VMEM], out_specs=(VMEM, VMEM)
    )(place, leaf_counts, occupancy, features, *near([others]))
    tables = neighbours, to_other_x(neighbours)
    biases = jnp.stack([bias_in, bias_out])
    biases = biases, to_other_core(biases)
    rims, (tables, biases), weights = gather_rims(place, tables, faces, (tables, biases), weight_in)
    rims, weight_out = lax.optimization_barrier((rims, weight_out))
    swapped = to_other_core(weight_out)
    parts, swapped = lax.optimization_barrier((conv(place, rows, rims, *weights), swapped))
    weights_out = split_weights(place, weight_out, swapped)
    parts = add_over_chips(parts)
    rows, faces = call(hidden_kernel, (close((512, 64)), close((192, 128))))(
        in_specs=[SMEM, SMEM] + [VMEM] * 11, out_specs=(VMEM, VMEM)
    )(place, leaf_counts, occupancy, *biases, *near(parts))

    rims, _, _ = gather_rims(place, tables, faces)
    parts = add_over_chips(conv(place, rows, rims, *weights_out))
    keep, give = call(result_kernel, (close((32, 512)), close((32, 512))))(
        in_specs=[SMEM, SMEM] + [VMEM] * 11, out_specs=(VMEM, VMEM)
    )(place, leaf_counts, occupancy, *biases, *near(parts))
    return call(merge_kernel, arr((32, 2, 512)))(in_specs=[SMEM, VMEM, VMEM], out_specs=VMEM)(
        place, *near([keep, to_other_core(give)])
    )


def solution(mesh):
    placed = (
        P("chan", "leaf", None),
        P("leaf"),
        P("leaf", None),
        P("leaf", None),
        P(None, "chan", None),
        P("chan"),
        P(None, "chan", None),
        P("chan"),
    )
    return jax.shard_map(
        body, mesh=mesh, in_specs=placed, out_specs=P("chan", "leaf", None), check_vma=False
    )
```

```python
import functools

import jax
import jax.numpy as jnp
from jax import lax
from jax.experimental import pallas as pl
from jax.experimental.pallas import tpu as pltpu
from jax.sharding import PartitionSpec as P

DIRECTIONS = [
    (first, second, third)
    for first in (-1, 0, 1)
    for second in (-1, 0, 1)
    for third in (-1, 0, 1)
    if (first, second, third) != (0, 0, 0)
]
VMEM = pl.BlockSpec(memory_space=pltpu.VMEM)
SMEM = pl.BlockSpec(memory_space=pltpu.SMEM)
F32 = jnp.float32
BF16 = jnp.bfloat16
ROWS = 24


def call(kernel, outs, scratch=(), flops=1000000, touched=1000000, room=16):
    return functools.partial(
        pl.pallas_call,
        kernel,
        out_shape=outs,
        scratch_shapes=list(scratch),
        compiler_params=pltpu.CompilerParams(vmem_limit_bytes=room * 1024 * 1024),
        cost_estimate=pl.CostEstimate(flops=flops, bytes_accessed=touched, transcendentals=0),
    )


def arr(shape, dtype=F32):
    return jax.ShapeDtypeStruct(shape, dtype)


def close(shape, dtype=F32):
    return pltpu.VMEM(shape, dtype)


def near(values):
    return [pltpu.with_memory_space_constraint(value, pltpu.VMEM) for value in values]


def weights_kernel(place, own, other, high, low):
    core = place[0]

    def step(tap, carry):
        mine, theirs = own[tap], other[tap]
        first = jnp.where(core == 0, mine, theirs)
        second = jnp.where(core == 0, theirs, mine)
        both = jnp.concatenate([first, second], axis=0)
        top = both.astype(BF16)
        high[tap] = top
        low[tap] = (both - top.astype(F32)).astype(BF16)
        return carry

    lax.fori_loop(0, 27, step, 0)


def split_weights(place, own, other):
    outs = (close((27, 64, 512), BF16), close((27, 64, 512), BF16))
    return call(weights_kernel, outs, flops=8000000, touched=9000000)(
        in_specs=[SMEM, VMEM, VMEM], out_specs=(VMEM, VMEM)
    )(place, own, other)


def cut_faces(rows, faces):
    faces[0:64, :] = jnp.concatenate([rows[0:64, :], rows[448:512, :]], axis=1)
    for x in range(8):
        faces[64 + 8 * x : 72 + 8 * x, :] = jnp.concatenate(
            [rows[64 * x : 64 * x + 8, :], rows[64 * x + 56 : 64 * x + 64, :]], axis=1
        )
    faces[128:192, :] = jnp.concatenate(
        [rows[pl.ds(0, 64, stride=8), :], rows[pl.ds(7, 64, stride=8), :]], axis=1
    )


def in_order(core, own, other):
    first = jnp.where(core == 0, own, other)
    second = jnp.where(core == 0, other, own)
    return jnp.concatenate([first, second], axis=0)


def active_voxels(core, counts, occupancy):
    chosen = jnp.where(core == 0, occupancy[0:1, :], occupancy[1:2, :]).astype(F32)
    return chosen * jnp.where(core < counts[0], 1.0, 0.0)


def features_kernel(place, counts, occupancy, own, other, rows, faces):
    core = place[0]
    mine = jnp.where(core == 0, own[:, 0, :], own[:, 1, :])
    theirs = jnp.where(core == 0, other[:, 0, :], other[:, 1, :])
    both = in_order(core, mine, theirs)
    rows[...] = (both * active_voxels(core, counts, occupancy)).T
    cut_faces(rows, faces)


def added(parts):
    value = parts[0][...]
    for part in parts[1:]:
        value = value + part[...]
    return value


def bias_row(core, own_bias, other_bias):
    own, other = own_bias[...], other_bias[...]
    first = jnp.where(core == 0, own, other)
    second = jnp.where(core == 0, other, own)
    return jnp.concatenate([first, second], axis=1)


def bias_column(row):
    wide = jnp.concatenate([row, row], axis=1)
    return jnp.broadcast_to(wide, (128, 128)).T[0:64, 0:1]


def hidden_kernel(place, counts, occupancy, own_bias, other_bias, *rest):
    core = place[0]
    rows, faces = rest[8:]
    bias = bias_column(bias_row(core, own_bias, other_bias))
    value = jnp.maximum(added(rest[:8]) + bias, 0.0)
    rows[...] = (value * active_voxels(core, counts, occupancy)).T
    cut_faces(rows, faces)


def result_kernel(place, counts, occupancy, own_bias, other_bias, *rest):
    core = place[0]
    keep, give = rest[8:]
    bias = bias_column(bias_row(core, own_bias, other_bias))
    value = (added(rest[:8]) + bias) * active_voxels(core, counts, occupancy)
    keep[...] = jnp.where(core == 0, value[0:32], value[32:64])
    give[...] = jnp.where(core == 0, value[32:64], value[0:32])


def merge_kernel(place, keep, got, out):
    core = place[0]
    out[:, 0, :] = jnp.where(core == 0, keep[...], got[...])
    out[:, 1, :] = jnp.where(core == 0, got[...], keep[...])


def rim_list():
    listed, begin = [], 192
    corner = 240
    for a, b, c in DIRECTIONS:
        steps = [step for step in (a, b, c) if step]
        if steps[0] < 0:
            continue
        if len(steps) == 1:
            listed.append(((a, b, c), 64 * (0 if a else (1 if b else 2)), 64))
        elif len(steps) == 2:
            listed.append(((a, b, c), begin, 8))
            begin += 8
        else:
            listed.append(((a, b, c), corner, 1))
            corner += 1
    return listed


RIM_ROWS = 248
SENT = (-1, 1, -2, 2, -3, 3, 4)


def face_rows(offsets):
    a, b, c = offsets
    y_at, z_at = (7 if b < 0 else 0), (7 if c < 0 else 0)
    if a:
        if b == 0:
            return pl.ds(0, 64) if c == 0 else pl.ds(z_at, 8, stride=8)
        return pl.ds(8 * y_at, 8) if c == 0 else pl.ds(8 * y_at + z_at, 1)
    if b:
        return pl.ds(64, 64) if c == 0 else pl.ds(64 + z_at, 8, stride=8)
    return pl.ds(128, 64)


def rims_kernel(place, own_table, other_table, *rest):
    blocks, outs, gathered = rest[:8], rest[8:12], rest[12]
    core, low_x, depth = place[0], place[1], place[2]
    for number, step in enumerate(SENT + (0,)):
        gathered[step % 8] = blocks[number][...]
    for peer in range(4):
        table = other_table if peer & 1 else own_table
        slot = core ^ (peer >> 1)
        out = outs[peer]
        out[240:248, :] = jnp.zeros((8, 128), F32)

        def load(offsets):
            entry = table[slot, DIRECTIONS.index(offsets)]
            found = jnp.clip(entry, 0, 31)
            here = (entry >= 0) & ((found & 1) == core) & (((found >> 1) & 1) == low_x)
            value = gathered[(depth - (found >> 2)) & 7, face_rows(offsets), :]
            return jnp.where(here, value, 0.0)

        for offsets, begin, count in rim_list():
            up, down = load(offsets), load(tuple(-step for step in offsets))
            lane = lax.broadcasted_iota(jnp.int32, (count, 128), 1)
            out[begin : begin + count, :] = jnp.where(lane < 64, up, down)


def cut_rims(place, own_table, other_table, blocks):
    outs = tuple(close((RIM_ROWS, 128)) for _ in range(4))
    return call(rims_kernel, outs, [pltpu.VMEM((8, 192, 128), F32)], touched=1000000)(
        in_specs=[SMEM, SMEM, SMEM] + [VMEM] * 8, out_specs=tuple([VMEM] * 4)
    )(place, own_table, other_table, *near(blocks))


def fill_rims(rims, padded):
    def at(x, y):
        return (x * 10 + y) * ROWS

    for upward, begin, count in rim_list():
        for sign in (1, -1):
            a, b, c = (sign * step for step in upward)
            side = 0 if sign > 0 else 64
            value = rims[begin : begin + count, side : side + 64]
            px, py = {-1: 0, 1: 9}.get(a), {-1: 0, 1: 9}.get(b)
            row = {-1: 7, 0: 8, 1: 16}[c]
            if count == 64:
                for n in range(8):
                    piece = value[8 * n : 8 * n + 8]
                    if a:
                        padded[pl.ds(at(px, 1 + n) + 8, 8), :] = piece
                    elif b:
                        padded[pl.ds(at(1 + n, py) + 8, 8), :] = piece
                    else:
                        padded[pl.ds(at(1 + n, 1) + row, 8, stride=ROWS), :] = piece
            elif count == 1:
                padded[pl.ds(at(px, py) + row, 1), :] = value
            elif c == 0:
                padded[pl.ds(at(px, py) + 8, 8), :] = value
            elif a:
                padded[pl.ds(at(px, 1) + row, 8, stride=ROWS), :] = value
            else:
                padded[pl.ds(at(1, py) + row, 8, stride=10 * ROWS), :] = value


def conv_kernel(place, rows, *rest):
    pieces = rest[:4]
    high, low = rest[4:6]
    outs = rest[6:14]
    rims, padded, columns, total, turned = rest[14:]
    rims[...] = (pieces[0][...] + pieces[1][...]) + (pieces[2][...] + pieces[3][...])
    for x in range(8):
        for y in range(8):
            padded[pl.ds(((1 + x) * 10 + 1 + y) * ROWS + 8, 8), :] = rows[pl.ds(x * 64 + y * 8, 8), :]
    fill_rims(rims, padded)
    for spot in range(100):
        before = padded[pl.ds(spot * ROWS + 7, 8), :]
        same = padded[pl.ds(spot * ROWS + 8, 8), :]
        after = padded[pl.ds(spot * ROWS + 9, 8), :]
        columns[spot // 10, spot % 10, :, 0:128] = jnp.concatenate([before, same], axis=1)
        columns[spot // 10, spot % 10, :, 128:192] = after

    dot = functools.partial(jnp.dot, preferred_element_type=F32)
    for p in range(3):
        sums = None
        for q in range(3):
            values = columns[p : p + 8, q : q + 8, :, 0:192].reshape(512, 192)
            top = values.astype(BF16)
            rest_of = (values - top.astype(F32)).astype(BF16)
            tap = 9 * p + 3 * q
            heavy = high[tap : tap + 3].reshape(192, 512)
            light = low[tap : tap + 3].reshape(192, 512)
            part = dot(top, heavy) + (dot(rest_of, heavy) + dot(top, light))
            sums = part if sums is None else sums + part
        if p == 0:
            total[...] = sums
        else:
            total[...] += sums
    turned[...] = total[...].T
    chip = place[3]
    for step, (along, across) in enumerate(ROUTES + ((0, 0),)):
        target = (((chip >> 1) + along) & 3) * 2 + ((chip & 1) ^ across)
        outs[step][...] = turned[pl.ds(pl.multiple_of(target * 64, 64), 64), :]


def conv(place, rows, rims, high, low):
    outs = tuple(close((64, 512)) for _ in range(8))
    scratch = [
        pltpu.VMEM((RIM_ROWS, 128), F32),
        pltpu.VMEM((100 * ROWS, 64), F32),
        pltpu.VMEM((10, 10, 8, 256), F32),
        pltpu.VMEM((512, 512), F32),
        pltpu.VMEM((512, 512), F32),
    ]
    return call(
        conv_kernel, outs, scratch, flops=2 * 3 * 1024 * 1728 * 256, touched=8000000, room=24
    )(
        in_specs=[SMEM] + [VMEM] * 7, out_specs=tuple([VMEM] * 8)
    )(place, *near([rows, *rims, high, low]))


def to_other_core(value):
    return lax.ppermute(value, "chan", [(i, i ^ 1) for i in range(16)])


def to_other_x(value):
    return lax.ppermute(value, "leaf", [(i, i ^ 1) for i in range(16)])


def to_other_both(value):
    pairs = [(16 * i + j, 16 * (i ^ 1) + (j ^ 1)) for i in range(16) for j in range(16)]
    return lax.ppermute(value, ("leaf", "chan"), pairs)


def gather_rims(place, tables, faces, weights=()):
    found = []
    for step in SENT:
        found.append(lax.ppermute(faces, "leaf", [(i, (i + 2 * step) % 16) for i in range(16)]))
    if weights:
        found, weights = lax.optimization_barrier((found, weights))
    own, beside, across, both = cut_rims(place, *tables, found + [faces])
    return [own, to_other_both(both), to_other_x(beside), to_other_core(across)], weights


def conv_beside(place, rows, rims, weights, moved):
    rims, moved = lax.optimization_barrier((rims, moved))
    parts = conv(place, rows, rims, *weights)
    return lax.optimization_barrier((parts, [to_other_core(value) for value in moved]))


ROUTES = ((2, 1), (1, 1), (3, 1), (2, 0), (0, 1), (1, 0), (3, 0))


def route_target(device, route):
    return (device // 4 + route[0]) % 4 * 4 + ((device % 4) ^ (2 * route[1]))


def add_over_chips(parts):
    landed = [parts[7]]
    for part, route in zip(parts, ROUTES):
        landed.append(lax.ppermute(part, "chan", [(i, route_target(i, route)) for i in range(16)]))
    return landed


def body(features, leaf_counts, occupancy, neighbours, weight_in, bias_in, weight_out, bias_out):
    leaf, chan = lax.axis_index("leaf"), lax.axis_index("chan")
    core = chan % 2
    place = jnp.stack([core, leaf % 2, leaf // 2, chan // 2]).astype(jnp.int32)
    others = to_other_core(features)
    rows, faces = call(features_kernel, (close((512, 64)), close((192, 128))))(
        in_specs=[SMEM, SMEM, VMEM, VMEM, VMEM], out_specs=(VMEM, VMEM)
    )(place, leaf_counts, occupancy, features, *near([others]))
    tables = neighbours, to_other_x(neighbours)
    bias_in, bias_out = bias_in.reshape(1, 32), bias_out.reshape(1, 32)
    weights = split_weights(place, weight_in, to_other_core(weight_in))

    rims, weights = gather_rims(place, tables, faces, weights)
    parts, (swapped, other_bias) = conv_beside(place, rows, rims, weights, [weight_out, bias_in])
    weights = split_weights(place, weight_out, swapped)
    parts = add_over_chips(parts)
    rows, faces = call(hidden_kernel, (close((512, 64)), close((192, 128))))(
        in_specs=[SMEM, SMEM] + [VMEM] * 11, out_specs=(VMEM, VMEM)
    )(place, leaf_counts, occupancy, bias_in, other_bias, *near(parts))

    rims, _ = gather_rims(place, tables, faces)
    parts, (other_bias,) = conv_beside(place, rows, rims, weights, [bias_out])
    parts = add_over_chips(parts)
    keep, give = call(result_kernel, (close((32, 512)), close((32, 512))))(
        in_specs=[SMEM, SMEM] + [VMEM] * 11, out_specs=(VMEM, VMEM)
    )(place, leaf_counts, occupancy, bias_out, other_bias, *near(parts))
    return call(merge_kernel, arr((32, 2, 512)))(in_specs=[SMEM, VMEM, VMEM], out_specs=VMEM)(
        place, *near([keep, to_other_core(give)])
    )


def solution(mesh):
    placed = (
        P("chan", "leaf", None),
        P("leaf"),
        P("leaf", None),
        P("leaf", None),
        P(None, "chan", None),
        P("chan"),
        P(None, "chan", None),
        P("chan"),
    )
    return jax.shard_map(
        body, mesh=mesh, in_specs=placed, out_specs=P("chan", "leaf", None), check_vma=False
    )
```

```python
import functools

import jax
import jax.numpy as jnp
from jax import lax
from jax.experimental import pallas as pl
from jax.experimental.pallas import tpu as pltpu
from jax.sharding import PartitionSpec as P

DIRECTIONS = [
    (first, second, third)
    for first in (-1, 0, 1)
    for second in (-1, 0, 1)
    for third in (-1, 0, 1)
    if (first, second, third) != (0, 0, 0)
]
VMEM = pl.BlockSpec(memory_space=pltpu.VMEM)
SMEM = pl.BlockSpec(memory_space=pltpu.SMEM)
F32 = jnp.float32
BF16 = jnp.bfloat16
ROWS = 24


def call(kernel, outs, scratch=(), flops=1000000, touched=1000000, room=16):
    return functools.partial(
        pl.pallas_call,
        kernel,
        out_shape=outs,
        scratch_shapes=list(scratch),
        compiler_params=pltpu.CompilerParams(vmem_limit_bytes=room * 1024 * 1024),
        cost_estimate=pl.CostEstimate(flops=flops, bytes_accessed=touched, transcendentals=0),
    )


def arr(shape, dtype=F32):
    return jax.ShapeDtypeStruct(shape, dtype)


def close(shape, dtype=F32):
    return pltpu.VMEM(shape, dtype)


def near(values):
    return [pltpu.with_memory_space_constraint(value, pltpu.VMEM) for value in values]


DEPTH = 3 * 9 * 64


def weights_kernel(place, own, other, stacked):
    core = place[0]
    for tap in range(27):
        p, q, r = tap // 9, tap // 3 % 3, tap % 3
        both = in_order(core, own[tap], other[tap])
        top = both.astype(BF16)
        low = (both - top.astype(F32)).astype(BF16)
        if r < 2:
            begin = 384 * q + 64 * r
            rows = (begin, begin + 128, begin + 256)
        else:
            rows = (1152 + 128 * q, 1216 + 128 * q, 1536 + 64 * q)
        for row, value in zip(rows, (top, top, low)):
            stacked[p, row : row + 64, :] = value


def split_weights(place, own, other):
    return call(weights_kernel, close((3, DEPTH, 512), BF16), flops=8000000, touched=9000000)(
        in_specs=[SMEM, VMEM, VMEM], out_specs=VMEM
    )(place, own, other)


def cut_faces(rows, faces):
    faces[0:64, :] = jnp.concatenate([rows[0:64, :], rows[448:512, :]], axis=1)
    for x in range(8):
        faces[64 + 8 * x : 72 + 8 * x, :] = jnp.concatenate(
            [rows[64 * x : 64 * x + 8, :], rows[64 * x + 56 : 64 * x + 64, :]], axis=1
        )
    faces[128:192, :] = jnp.concatenate(
        [rows[pl.ds(0, 64, stride=8), :], rows[pl.ds(7, 64, stride=8), :]], axis=1
    )


def in_order(core, own, other):
    first = jnp.where(core == 0, own, other)
    second = jnp.where(core == 0, other, own)
    return jnp.concatenate([first, second], axis=0)


def active_voxels(core, counts, occupancy):
    chosen = jnp.where(core == 0, occupancy[0:1, :], occupancy[1:2, :]).astype(F32)
    return chosen * jnp.where(core < counts[0], 1.0, 0.0)


def features_kernel(place, counts, occupancy, own, other, rows, faces):
    core = place[0]
    mine = jnp.where(core == 0, own[:, 0, :], own[:, 1, :])
    theirs = jnp.where(core == 0, other[:, 0, :], other[:, 1, :])
    both = in_order(core, mine, theirs)
    rows[...] = (both * active_voxels(core, counts, occupancy)).T
    cut_faces(rows, faces)


def added(parts):
    value = parts[0][...]
    for part in parts[1:]:
        value = value + part[...]
    return value


def bias_row(core, own_bias, other_bias):
    own, other = own_bias[...], other_bias[...]
    first = jnp.where(core == 0, own, other)
    second = jnp.where(core == 0, other, own)
    return jnp.concatenate([first, second], axis=1)


def bias_column(row):
    wide = jnp.concatenate([row, row], axis=1)
    return jnp.broadcast_to(wide, (128, 128)).T[0:64, 0:1]


def hidden_kernel(place, counts, occupancy, own_bias, other_bias, *rest):
    core = place[0]
    rows, faces = rest[8:]
    bias = bias_column(bias_row(core, own_bias, other_bias))
    value = jnp.maximum(added(rest[:8]) + bias, 0.0)
    rows[...] = (value * active_voxels(core, counts, occupancy)).T
    cut_faces(rows, faces)


def result_kernel(place, counts, occupancy, own_bias, other_bias, *rest):
    core = place[0]
    keep, give = rest[8:]
    bias = bias_column(bias_row(core, own_bias, other_bias))
    value = (added(rest[:8]) + bias) * active_voxels(core, counts, occupancy)
    keep[...] = jnp.where(core == 0, value[0:32], value[32:64])
    give[...] = jnp.where(core == 0, value[32:64], value[0:32])


def merge_kernel(place, keep, got, out):
    core = place[0]
    out[:, 0, :] = jnp.where(core == 0, keep[...], got[...])
    out[:, 1, :] = jnp.where(core == 0, got[...], keep[...])


def rim_list():
    listed, begin = [], 192
    corner = 240
    for a, b, c in DIRECTIONS:
        steps = [step for step in (a, b, c) if step]
        if steps[0] < 0:
            continue
        if len(steps) == 1:
            listed.append(((a, b, c), 64 * (0 if a else (1 if b else 2)), 64))
        elif len(steps) == 2:
            listed.append(((a, b, c), begin, 8))
            begin += 8
        else:
            listed.append(((a, b, c), corner, 1))
            corner += 1
    return listed


RIM_ROWS = 248
SENT = (-1, 1, -2, 2, -3, 3, 4)


def face_rows(offsets):
    a, b, c = offsets
    y_at, z_at = (7 if b < 0 else 0), (7 if c < 0 else 0)
    if a:
        if b == 0:
            return pl.ds(0, 64) if c == 0 else pl.ds(z_at, 8, stride=8)
        return pl.ds(8 * y_at, 8) if c == 0 else pl.ds(8 * y_at + z_at, 1)
    if b:
        return pl.ds(64, 64) if c == 0 else pl.ds(64 + z_at, 8, stride=8)
    return pl.ds(128, 64)


def rims_kernel(place, own_table, other_table, *rest):
    blocks, outs, gathered = rest[:8], rest[8:12], rest[12]
    core, low_x, depth = place[0], place[1], place[2]
    for number, step in enumerate(SENT + (0,)):
        gathered[step % 8] = blocks[number][...]
    for peer in range(4):
        table = other_table if peer & 1 else own_table
        slot = core ^ (peer >> 1)
        out = outs[peer]
        out[240:248, :] = jnp.zeros((8, 128), F32)

        def load(offsets):
            entry = table[slot, DIRECTIONS.index(offsets)]
            found = jnp.clip(entry, 0, 31)
            here = (entry >= 0) & ((found & 1) == core) & (((found >> 1) & 1) == low_x)
            value = gathered[(depth - (found >> 2)) & 7, face_rows(offsets), :]
            return jnp.where(here, value, 0.0)

        for offsets, begin, count in rim_list():
            up, down = load(offsets), load(tuple(-step for step in offsets))
            lane = lax.broadcasted_iota(jnp.int32, (count, 128), 1)
            out[begin : begin + count, :] = jnp.where(lane < 64, up, down)


def cut_rims(place, own_table, other_table, blocks):
    outs = tuple(close((RIM_ROWS, 128)) for _ in range(4))
    return call(rims_kernel, outs, [pltpu.VMEM((8, 192, 128), F32)], touched=1000000)(
        in_specs=[SMEM, SMEM, SMEM] + [VMEM] * 8, out_specs=tuple([VMEM] * 4)
    )(place, own_table, other_table, *near(blocks))


def fill_rims(rims, padded):
    def at(x, y):
        return (x * 10 + y) * ROWS

    for upward, begin, count in rim_list():
        for sign in (1, -1):
            a, b, c = (sign * step for step in upward)
            side = 0 if sign > 0 else 64
            value = rims[begin : begin + count, side : side + 64]
            px, py = {-1: 0, 1: 9}.get(a), {-1: 0, 1: 9}.get(b)
            row = {-1: 7, 0: 8, 1: 16}[c]
            if count == 64:
                for n in range(8):
                    piece = value[8 * n : 8 * n + 8]
                    if a:
                        padded[pl.ds(at(px, 1 + n) + 8, 8), :] = piece
                    elif b:
                        padded[pl.ds(at(1 + n, py) + 8, 8), :] = piece
                    else:
                        padded[pl.ds(at(1 + n, 1) + row, 8, stride=ROWS), :] = piece
            elif count == 1:
                padded[pl.ds(at(px, py) + row, 1), :] = value
            elif c == 0:
                padded[pl.ds(at(px, py) + 8, 8), :] = value
            elif a:
                padded[pl.ds(at(px, 1) + row, 8, stride=ROWS), :] = value
            else:
                padded[pl.ds(at(1, py) + row, 8, stride=10 * ROWS), :] = value


def conv_kernel(place, rows, *rest):
    pieces = rest[:4]
    stacked = rest[4]
    outs = rest[5:13]
    rims, padded, columns, total, turned = rest[13:]
    rims[...] = (pieces[0][...] + pieces[1][...]) + (pieces[2][...] + pieces[3][...])
    for x in range(8):
        for y in range(8):
            padded[pl.ds(((1 + x) * 10 + 1 + y) * ROWS + 8, 8), :] = rows[pl.ds(x * 64 + y * 8, 8), :]
    fill_rims(rims, padded)
    for spot in range(100):
        before = padded[pl.ds(spot * ROWS + 7, 8), :]
        same = padded[pl.ds(spot * ROWS + 8, 8), :]
        after = padded[pl.ds(spot * ROWS + 9, 8), :]
        columns[spot // 10, spot % 10, :, 0:128] = jnp.concatenate([before, same], axis=1)
        columns[spot // 10, spot % 10, :, 128:192] = after

    for p in range(3):
        firsts, pairs, tails = [], [], []
        for q in range(3):
            values = columns[p : p + 8, q : q + 8, :, 0:192].reshape(512, 192)
            top = values.astype(BF16).astype(F32)
            low = values - top
            firsts += [top[:, 0:128], low[:, 0:128], top[:, 0:128]]
            pairs.append(jnp.concatenate([top[:, 128:192], low[:, 128:192]], axis=1))
            tails.append(top[:, 128:192])
        ends = [jnp.concatenate(tails[:2], axis=1), tails[2]]
        left = jnp.concatenate([piece.astype(BF16) for piece in firsts + pairs + ends], axis=1)
        sums = jnp.dot(left, stacked[p], preferred_element_type=F32)
        if p == 0:
            total[...] = sums
        else:
            total[...] += sums
    turned[...] = total[...].T
    chip = place[3]
    for step, (along, across) in enumerate(ROUTES + ((0, 0),)):
        target = (((chip >> 1) + along) & 3) * 2 + ((chip & 1) ^ across)
        outs[step][...] = turned[pl.ds(pl.multiple_of(target * 64, 64), 64), :]


def conv(place, rows, rims, stacked):
    outs = tuple(close((64, 512)) for _ in range(8))
    scratch = [
        pltpu.VMEM((RIM_ROWS, 128), F32),
        pltpu.VMEM((100 * ROWS, 64), F32),
        pltpu.VMEM((10, 10, 8, 256), F32),
        pltpu.VMEM((512, 512), F32),
        pltpu.VMEM((512, 512), F32),
    ]
    return call(
        conv_kernel, outs, scratch, flops=2 * 3 * 1024 * 1728 * 256, touched=8000000, room=24
    )(
        in_specs=[SMEM] + [VMEM] * 6, out_specs=tuple([VMEM] * 8)
    )(place, *near([rows, *rims, stacked]))


def to_other_core(value):
    return lax.ppermute(value, "chan", [(i, i ^ 1) for i in range(16)])


def to_other_x(value):
    return lax.ppermute(value, "leaf", [(i, i ^ 1) for i in range(16)])


def to_other_both(value):
    pairs = [(16 * i + j, 16 * (i ^ 1) + (j ^ 1)) for i in range(16) for j in range(16)]
    return lax.ppermute(value, ("leaf", "chan"), pairs)


def gather_rims(place, tables, faces, weights=None):
    found = []
    for step in SENT:
        found.append(lax.ppermute(faces, "leaf", [(i, (i + 2 * step) % 16) for i in range(16)]))
    if weights is not None:
        found, weights = lax.optimization_barrier((found, weights))
    own, beside, across, both = cut_rims(place, *tables, found + [faces])
    return [own, to_other_both(both), to_other_x(beside), to_other_core(across)], weights


def conv_beside(place, rows, rims, weights, moved):
    rims, moved = lax.optimization_barrier((rims, moved))
    parts = conv(place, rows, rims, weights)
    return lax.optimization_barrier((parts, [to_other_core(value) for value in moved]))


ROUTES = ((2, 1), (1, 1), (3, 1), (2, 0), (0, 1), (1, 0), (3, 0))


def route_target(device, route):
    return (device // 4 + route[0]) % 4 * 4 + ((device % 4) ^ (2 * route[1]))


def add_over_chips(parts):
    landed = [parts[7]]
    for part, route in zip(parts, ROUTES):
        landed.append(lax.ppermute(part, "chan", [(i, route_target(i, route)) for i in range(16)]))
    return landed


def body(features, leaf_counts, occupancy, neighbours, weight_in, bias_in, weight_out, bias_out):
    leaf, chan = lax.axis_index("leaf"), lax.axis_index("chan")
    core = chan % 2
    place = jnp.stack([core, leaf % 2, leaf // 2, chan // 2]).astype(jnp.int32)
    place, weight_in = lax.optimization_barrier((place, weight_in))
    others = to_other_core(features)
    rows, faces = call(features_kernel, (close((512, 64)), close((192, 128))))(
        in_specs=[SMEM, SMEM, VMEM, VMEM, VMEM], out_specs=(VMEM, VMEM)
    )(place, leaf_counts, occupancy, features, *near([others]))
    tables = neighbours, to_other_x(neighbours)
    bias_in, bias_out = bias_in.reshape(1, 32), bias_out.reshape(1, 32)
    swapped, tables = lax.optimization_barrier((to_other_core(weight_in), tables))
    weights = split_weights(place, weight_in, swapped)

    rims, weights = gather_rims(place, tables, faces, weights)
    parts, (swapped, other_bias) = conv_beside(place, rows, rims, weights, [weight_out, bias_in])
    weights = split_weights(place, weight_out, swapped)
    parts = add_over_chips(parts)
    rows, faces = call(hidden_kernel, (close((512, 64)), close((192, 128))))(
        in_specs=[SMEM, SMEM] + [VMEM] * 11, out_specs=(VMEM, VMEM)
    )(place, leaf_counts, occupancy, bias_in, other_bias, *near(parts))

    rims, _ = gather_rims(place, tables, faces)
    parts, (other_bias,) = conv_beside(place, rows, rims, weights, [bias_out])
    parts = add_over_chips(parts)
    keep, give = call(result_kernel, (close((32, 512)), close((32, 512))))(
        in_specs=[SMEM, SMEM] + [VMEM] * 11, out_specs=(VMEM, VMEM)
    )(place, leaf_counts, occupancy, bias_out, other_bias, *near(parts))
    return call(merge_kernel, arr((32, 2, 512)))(in_specs=[SMEM, VMEM, VMEM], out_specs=VMEM)(
        place, *near([keep, to_other_core(give)])
    )


def solution(mesh):
    placed = (
        P("chan", "leaf", None),
        P("leaf"),
        P("leaf", None),
        P("leaf", None),
        P(None, "chan", None),
        P("chan"),
        P(None, "chan", None),
        P("chan"),
    )
    return jax.shard_map(
        body, mesh=mesh, in_specs=placed, out_specs=P("chan", "leaf", None), check_vma=False
    )
```

```python
import functools

import jax
import jax.numpy as jnp
from jax import lax
from jax.experimental import pallas as pl
from jax.experimental.pallas import tpu as pltpu
from jax.sharding import PartitionSpec as P

DIRECTIONS = [
    (first, second, third)
    for first in (-1, 0, 1)
    for second in (-1, 0, 1)
    for third in (-1, 0, 1)
    if (first, second, third) != (0, 0, 0)
]
VMEM = pl.BlockSpec(memory_space=pltpu.VMEM)
SMEM = pl.BlockSpec(memory_space=pltpu.SMEM)
F32 = jnp.float32
BF16 = jnp.bfloat16
ROWS = 24


def call(kernel, outs, scratch=(), flops=1000000, touched=1000000, room=16):
    return functools.partial(
        pl.pallas_call,
        kernel,
        out_shape=outs,
        scratch_shapes=list(scratch),
        compiler_params=pltpu.CompilerParams(vmem_limit_bytes=room * 1024 * 1024),
        cost_estimate=pl.CostEstimate(flops=flops, bytes_accessed=touched, transcendentals=0),
    )


def arr(shape, dtype=F32):
    return jax.ShapeDtypeStruct(shape, dtype)


def close(shape, dtype=F32):
    return pltpu.VMEM(shape, dtype)


def near(values):
    return [pltpu.with_memory_space_constraint(value, pltpu.VMEM) for value in values]


DEPTH = 3 * 9 * 64


def weights_kernel(place, own, other, stacked):
    core = place[0]
    for tap in range(27):
        p, q, r = tap // 9, tap // 3 % 3, tap % 3
        both = in_order(core, own[tap], other[tap])
        top = both.astype(BF16)
        low = (both - top.astype(F32)).astype(BF16)
        if r < 2:
            begin = 384 * q + 64 * r
            rows = (begin, begin + 128, begin + 256)
        else:
            rows = (1152 + 128 * q, 1216 + 128 * q, 1536 + 64 * q)
        for row, value in zip(rows, (top, top, low)):
            stacked[p, row : row + 64, :] = value


def split_weights(place, own, other):
    return call(weights_kernel, close((3, DEPTH, 512), BF16), flops=8000000, touched=9000000)(
        in_specs=[SMEM, VMEM, VMEM], out_specs=VMEM
    )(place, own, other)


def cut_faces(rows, faces):
    faces[0:64, :] = jnp.concatenate([rows[0:64, :], rows[448:512, :]], axis=1)
    for x in range(8):
        faces[64 + 8 * x : 72 + 8 * x, :] = jnp.concatenate(
            [rows[64 * x : 64 * x + 8, :], rows[64 * x + 56 : 64 * x + 64, :]], axis=1
        )
    faces[128:192, :] = jnp.concatenate(
        [rows[pl.ds(0, 64, stride=8), :], rows[pl.ds(7, 64, stride=8), :]], axis=1
    )


def in_order(core, own, other):
    first = jnp.where(core == 0, own, other)
    second = jnp.where(core == 0, other, own)
    return jnp.concatenate([first, second], axis=0)


def active_voxels(core, counts, occupancy):
    chosen = jnp.where(core == 0, occupancy[0:1, :], occupancy[1:2, :]).astype(F32)
    return chosen * jnp.where(core < counts[0], 1.0, 0.0)


def own_kernel(place, counts, occupancy, own, masked, active):
    core = place[0]
    active[...] = active_voxels(core, counts, occupancy)
    masked[...] = jnp.where(core == 0, own[:, 0, :], own[:, 1, :]) * active[...]


def features_kernel(place, masked, active, other, rows, faces):
    core = place[0]
    theirs = jnp.where(core == 0, other[:, 0, :], other[:, 1, :]) * active[...]
    rows[...] = in_order(core, masked[...], theirs).T
    cut_faces(rows, faces)


def added(parts):
    value = parts[0][...]
    for part in parts[1:]:
        value = value + part[...]
    return value


def bias_row(core, own_bias, other_bias):
    own, other = own_bias[...], other_bias[...]
    first = jnp.where(core == 0, own, other)
    second = jnp.where(core == 0, other, own)
    return jnp.concatenate([first, second], axis=1)


def bias_column(row):
    wide = jnp.concatenate([row, row], axis=1)
    return jnp.broadcast_to(wide, (128, 128)).T[0:64, 0:1]


def hidden_kernel(place, counts, occupancy, own_bias, other_bias, *rest):
    core = place[0]
    rows, faces = rest[8:]
    bias = bias_column(bias_row(core, own_bias, other_bias))
    value = jnp.maximum(added(rest[:8]) + bias, 0.0)
    rows[...] = (value * active_voxels(core, counts, occupancy)).T
    cut_faces(rows, faces)


def result_kernel(place, counts, occupancy, own_bias, other_bias, *rest):
    core = place[0]
    keep, give = rest[8:]
    bias = bias_column(bias_row(core, own_bias, other_bias))
    value = (added(rest[:8]) + bias) * active_voxels(core, counts, occupancy)
    keep[...] = jnp.where(core == 0, value[0:32], value[32:64])
    give[...] = jnp.where(core == 0, value[32:64], value[0:32])


def merge_kernel(place, keep, got, out):
    core = place[0]
    out[:, 0, :] = jnp.where(core == 0, keep[...], got[...])
    out[:, 1, :] = jnp.where(core == 0, got[...], keep[...])


def rim_list():
    listed, begin = [], 192
    corner = 240
    for a, b, c in DIRECTIONS:
        steps = [step for step in (a, b, c) if step]
        if steps[0] < 0:
            continue
        if len(steps) == 1:
            listed.append(((a, b, c), 64 * (0 if a else (1 if b else 2)), 64))
        elif len(steps) == 2:
            listed.append(((a, b, c), begin, 8))
            begin += 8
        else:
            listed.append(((a, b, c), corner, 1))
            corner += 1
    return listed


RIM_ROWS = 248
SENT = (-1, 1, -2, 2, -3, 3, 4)


def face_rows(offsets):
    a, b, c = offsets
    y_at, z_at = (7 if b < 0 else 0), (7 if c < 0 else 0)
    if a:
        if b == 0:
            return pl.ds(0, 64) if c == 0 else pl.ds(z_at, 8, stride=8)
        return pl.ds(8 * y_at, 8) if c == 0 else pl.ds(8 * y_at + z_at, 1)
    if b:
        return pl.ds(64, 64) if c == 0 else pl.ds(64 + z_at, 8, stride=8)
    return pl.ds(128, 64)


def rims_kernel(place, own_table, other_table, *rest):
    blocks, outs, gathered = rest[:8], rest[8:12], rest[12]
    core, low_x, depth = place[0], place[1], place[2]
    for number, step in enumerate(SENT + (0,)):
        gathered[step % 8] = blocks[number][...]
    for peer in range(4):
        table = other_table if peer & 1 else own_table
        slot = core ^ (peer >> 1)
        out = outs[peer]
        out[240:248, :] = jnp.zeros((8, 128), F32)

        def load(offsets):
            entry = table[slot, DIRECTIONS.index(offsets)]
            found = jnp.clip(entry, 0, 31)
            here = (entry >= 0) & ((found & 1) == core) & (((found >> 1) & 1) == low_x)
            value = gathered[(depth - (found >> 2)) & 7, face_rows(offsets), :]
            return jnp.where(here, value, 0.0)

        for offsets, begin, count in rim_list():
            up, down = load(offsets), load(tuple(-step for step in offsets))
            lane = lax.broadcasted_iota(jnp.int32, (count, 128), 1)
            out[begin : begin + count, :] = jnp.where(lane < 64, up, down)


def cut_rims(place, own_table, other_table, blocks):
    outs = tuple(close((RIM_ROWS, 128)) for _ in range(4))
    return call(rims_kernel, outs, [pltpu.VMEM((8, 192, 128), F32)], touched=1000000)(
        in_specs=[SMEM, SMEM, SMEM] + [VMEM] * 8, out_specs=tuple([VMEM] * 4)
    )(place, own_table, other_table, *near(blocks))


def fill_rims(rims, padded):
    def at(x, y):
        return (x * 10 + y) * ROWS

    for upward, begin, count in rim_list():
        for sign in (1, -1):
            a, b, c = (sign * step for step in upward)
            side = 0 if sign > 0 else 64
            value = rims[begin : begin + count, side : side + 64]
            px, py = {-1: 0, 1: 9}.get(a), {-1: 0, 1: 9}.get(b)
            row = {-1: 7, 0: 8, 1: 16}[c]
            if count == 64:
                for n in range(8):
                    piece = value[8 * n : 8 * n + 8]
                    if a:
                        padded[pl.ds(at(px, 1 + n) + 8, 8), :] = piece
                    elif b:
                        padded[pl.ds(at(1 + n, py) + 8, 8), :] = piece
                    else:
                        padded[pl.ds(at(1 + n, 1) + row, 8, stride=ROWS), :] = piece
            elif count == 1:
                padded[pl.ds(at(px, py) + row, 1), :] = value
            elif c == 0:
                padded[pl.ds(at(px, py) + 8, 8), :] = value
            elif a:
                padded[pl.ds(at(px, 1) + row, 8, stride=ROWS), :] = value
            else:
                padded[pl.ds(at(1, py) + row, 8, stride=10 * ROWS), :] = value


def conv_kernel(place, rows, *rest):
    pieces = rest[:4]
    stacked = rest[4]
    outs = rest[5:13]
    rims, padded, columns, total, turned = rest[13:]
    rims[...] = (pieces[0][...] + pieces[1][...]) + (pieces[2][...] + pieces[3][...])
    for x in range(8):
        for y in range(8):
            padded[pl.ds(((1 + x) * 10 + 1 + y) * ROWS + 8, 8), :] = rows[pl.ds(x * 64 + y * 8, 8), :]
    fill_rims(rims, padded)
    for spot in range(100):
        before = padded[pl.ds(spot * ROWS + 7, 8), :]
        same = padded[pl.ds(spot * ROWS + 8, 8), :]
        after = padded[pl.ds(spot * ROWS + 9, 8), :]
        columns[spot // 10, spot % 10, :, 0:128] = jnp.concatenate([before, same], axis=1)
        columns[spot // 10, spot % 10, :, 128:192] = after

    for p in range(3):
        firsts, pairs, tails = [], [], []
        for q in range(3):
            values = columns[p : p + 8, q : q + 8, :, 0:192].reshape(512, 192)
            top = values.astype(BF16).astype(F32)
            low = values - top
            firsts += [top[:, 0:128], low[:, 0:128], top[:, 0:128]]
            pairs.append(jnp.concatenate([top[:, 128:192], low[:, 128:192]], axis=1))
            tails.append(top[:, 128:192])
        ends = [jnp.concatenate(tails[:2], axis=1), tails[2]]
        left = jnp.concatenate([piece.astype(BF16) for piece in firsts + pairs + ends], axis=1)
        sums = jnp.dot(left, stacked[p], preferred_element_type=F32)
        if p == 0:
            total[...] = sums
        else:
            total[...] += sums
    turned[...] = total[...].T
    chip = place[3]
    for step, (along, across) in enumerate(ROUTES + ((0, 0),)):
        target = (((chip >> 1) + along) & 3) * 2 + ((chip & 1) ^ across)
        outs[step][...] = turned[pl.ds(pl.multiple_of(target * 64, 64), 64), :]


def conv(place, rows, rims, stacked):
    outs = tuple(close((64, 512)) for _ in range(8))
    scratch = [
        pltpu.VMEM((RIM_ROWS, 128), F32),
        pltpu.VMEM((100 * ROWS, 64), F32),
        pltpu.VMEM((10, 10, 8, 256), F32),
        pltpu.VMEM((512, 512), F32),
        pltpu.VMEM((512, 512), F32),
    ]
    return call(
        conv_kernel, outs, scratch, flops=2 * 3 * 1024 * 1728 * 256, touched=8000000, room=24
    )(
        in_specs=[SMEM] + [VMEM] * 6, out_specs=tuple([VMEM] * 8)
    )(place, *near([rows, *rims, stacked]))


def to_other_core(value):
    return lax.ppermute(value, "chan", [(i, i ^ 1) for i in range(16)])


def to_other_x(value):
    return lax.ppermute(value, "leaf", [(i, i ^ 1) for i in range(16)])


def to_other_both(value):
    pairs = [(16 * i + j, 16 * (i ^ 1) + (j ^ 1)) for i in range(16) for j in range(16)]
    return lax.ppermute(value, ("leaf", "chan"), pairs)


def gather_rims(place, tables, faces, weights=None):
    found = []
    for step in SENT:
        found.append(lax.ppermute(faces, "leaf", [(i, (i + 2 * step) % 16) for i in range(16)]))
    if weights is not None:
        found, weights = lax.optimization_barrier((found, weights))
    own, beside, across, both = cut_rims(place, *tables, found + [faces])
    return [own, to_other_both(both), to_other_x(beside), to_other_core(across)], weights


def conv_beside(place, rows, rims, weights, moved):
    rims, moved = lax.optimization_barrier((rims, moved))
    parts = conv(place, rows, rims, weights)
    return lax.optimization_barrier((parts, [to_other_core(value) for value in moved]))


ROUTES = ((2, 1), (1, 1), (3, 1), (2, 0), (0, 1), (1, 0), (3, 0))


def route_target(device, route):
    return (device // 4 + route[0]) % 4 * 4 + ((device % 4) ^ (2 * route[1]))


def add_over_chips(parts):
    landed = [parts[7]]
    for part, route in zip(parts, ROUTES):
        landed.append(lax.ppermute(part, "chan", [(i, route_target(i, route)) for i in range(16)]))
    return landed


def body(features, leaf_counts, occupancy, neighbours, weight_in, bias_in, weight_out, bias_out):
    leaf, chan = lax.axis_index("leaf"), lax.axis_index("chan")
    core = chan % 2
    place = jnp.stack([core, leaf % 2, leaf // 2, chan // 2]).astype(jnp.int32)
    place, weight_in = lax.optimization_barrier((place, weight_in))
    others = to_other_core(features)
    masked, active = call(own_kernel, (close((32, 512)), close((1, 512))))(
        in_specs=[SMEM, SMEM, VMEM, VMEM], out_specs=(VMEM, VMEM)
    )(place, leaf_counts, occupancy, features)
    rows, faces = call(features_kernel, (close((512, 64)), close((192, 128))))(
        in_specs=[SMEM, VMEM, VMEM, VMEM], out_specs=(VMEM, VMEM)
    )(place, *near([masked, active, others]))
    tables = neighbours, to_other_x(neighbours)
    bias_in, bias_out = bias_in.reshape(1, 32), bias_out.reshape(1, 32)
    swapped, tables = lax.optimization_barrier((to_other_core(weight_in), tables))
    weights = split_weights(place, weight_in, swapped)

    rims, weights = gather_rims(place, tables, faces, weights)
    parts, (swapped, other_bias) = conv_beside(place, rows, rims, weights, [weight_out, bias_in])
    weights = split_weights(place, weight_out, swapped)
    parts = add_over_chips(parts)
    rows, faces = call(hidden_kernel, (close((512, 64)), close((192, 128))))(
        in_specs=[SMEM, SMEM] + [VMEM] * 11, out_specs=(VMEM, VMEM)
    )(place, leaf_counts, occupancy, bias_in, other_bias, *near(parts))

    rims, _ = gather_rims(place, tables, faces)
    parts, (other_bias,) = conv_beside(place, rows, rims, weights, [bias_out])
    parts = add_over_chips(parts)
    keep, give = call(result_kernel, (close((32, 512)), close((32, 512))))(
        in_specs=[SMEM, SMEM] + [VMEM] * 11, out_specs=(VMEM, VMEM)
    )(place, leaf_counts, occupancy, bias_out, other_bias, *near(parts))
    return call(merge_kernel, arr((32, 2, 512)))(in_specs=[SMEM, VMEM, VMEM], out_specs=VMEM)(
        place, *near([keep, to_other_core(give)])
    )


def solution(mesh):
    placed = (
        P("chan", "leaf", None),
        P("leaf"),
        P("leaf", None),
        P("leaf", None),
        P(None, "chan", None),
        P("chan"),
        P(None, "chan", None),
        P("chan"),
    )
    return jax.shard_map(
        body, mesh=mesh, in_specs=placed, out_specs=P("chan", "leaf", None), check_vma=False
    )
```

```python
import functools

import jax
import jax.numpy as jnp
from jax import lax
from jax.experimental import pallas as pl
from jax.experimental.pallas import tpu as pltpu
from jax.sharding import PartitionSpec as P

DIRECTIONS = [
    (first, second, third)
    for first in (-1, 0, 1)
    for second in (-1, 0, 1)
    for third in (-1, 0, 1)
    if (first, second, third) != (0, 0, 0)
]
VMEM = pl.BlockSpec(memory_space=pltpu.VMEM)
SMEM = pl.BlockSpec(memory_space=pltpu.SMEM)
F32 = jnp.float32
BF16 = jnp.bfloat16
ROWS = 24


def call(kernel, outs, scratch=(), flops=1000000, touched=1000000, room=16):
    return functools.partial(
        pl.pallas_call,
        kernel,
        out_shape=outs,
        scratch_shapes=list(scratch),
        compiler_params=pltpu.CompilerParams(vmem_limit_bytes=room * 1024 * 1024),
        cost_estimate=pl.CostEstimate(flops=flops, bytes_accessed=touched, transcendentals=0),
    )


def arr(shape, dtype=F32):
    return jax.ShapeDtypeStruct(shape, dtype)


def close(shape, dtype=F32):
    return pltpu.VMEM(shape, dtype)


def near(values):
    return [pltpu.with_memory_space_constraint(value, pltpu.VMEM) for value in values]


DEPTH = 3 * 9 * 64


def weights_kernel(place, own, other, stacked):
    core = place[0]
    for tap in range(27):
        p, q, r = tap // 9, tap // 3 % 3, tap % 3
        both = in_order(core, own[tap], other[tap])
        top = both.astype(BF16)
        low = (both - top.astype(F32)).astype(BF16)
        if r < 2:
            begin = 384 * q + 64 * r
            rows = (begin, begin + 128, begin + 256)
        else:
            rows = (1152 + 128 * q, 1216 + 128 * q, 1536 + 64 * q)
        for row, value in zip(rows, (top, top, low)):
            stacked[p, row : row + 64, :] = value


def split_weights(place, own, other):
    return call(weights_kernel, close((3, DEPTH, 512), BF16), flops=8000000, touched=9000000)(
        in_specs=[SMEM, VMEM, VMEM], out_specs=VMEM
    )(place, own, other)


def cut_faces(rows, faces):
    faces[0:64, :] = jnp.concatenate([rows[0:64, :], rows[448:512, :]], axis=1)
    for x in range(8):
        faces[64 + 8 * x : 72 + 8 * x, :] = jnp.concatenate(
            [rows[64 * x : 64 * x + 8, :], rows[64 * x + 56 : 64 * x + 64, :]], axis=1
        )
    faces[128:192, :] = jnp.concatenate(
        [rows[pl.ds(0, 64, stride=8), :], rows[pl.ds(7, 64, stride=8), :]], axis=1
    )


def in_order(core, own, other):
    first = jnp.where(core == 0, own, other)
    second = jnp.where(core == 0, other, own)
    return jnp.concatenate([first, second], axis=0)


def active_voxels(core, counts, occupancy):
    chosen = jnp.where(core == 0, occupancy[0:1, :], occupancy[1:2, :]).astype(F32)
    return chosen * jnp.where(core < counts[0], 1.0, 0.0)


def own_kernel(place, counts, occupancy, own, masked, active):
    core = place[0]
    active[...] = active_voxels(core, counts, occupancy)
    masked[...] = jnp.where(core == 0, own[:, 0, :], own[:, 1, :]) * active[...]


def features_kernel(place, masked, active, other, rows, faces):
    core = place[0]
    theirs = jnp.where(core == 0, other[:, 0, :], other[:, 1, :]) * active[...]
    rows[...] = in_order(core, masked[...], theirs).T
    cut_faces(rows, faces)


def added(parts):
    value = parts[0][...]
    for part in parts[1:]:
        value = value + part[...]
    return value


def bias_row(core, own_bias, other_bias):
    own, other = own_bias[...], other_bias[...]
    first = jnp.where(core == 0, own, other)
    second = jnp.where(core == 0, other, own)
    return jnp.concatenate([first, second], axis=1)


def bias_column(row):
    wide = jnp.concatenate([row, row], axis=1)
    return jnp.broadcast_to(wide, (128, 128)).T[0:64, 0:1]


def hidden_kernel(place, counts, occupancy, own_bias, other_bias, *rest):
    core = place[0]
    rows, faces = rest[8:]
    bias = bias_column(bias_row(core, own_bias, other_bias))
    value = jnp.maximum(added(rest[:8]) + bias, 0.0)
    rows[...] = (value * active_voxels(core, counts, occupancy)).T
    cut_faces(rows, faces)


def result_kernel(place, counts, occupancy, own_bias, other_bias, *rest):
    core = place[0]
    keep, give = rest[8:]
    bias = bias_column(bias_row(core, own_bias, other_bias))
    value = (added(rest[:8]) + bias) * active_voxels(core, counts, occupancy)
    keep[...] = jnp.where(core == 0, value[0:32], value[32:64])
    give[...] = jnp.where(core == 0, value[32:64], value[0:32])


def merge_kernel(place, keep, got, out):
    core = place[0]
    out[:, 0, :] = jnp.where(core == 0, keep[...], got[...])
    out[:, 1, :] = jnp.where(core == 0, got[...], keep[...])


def rim_list():
    listed, begin = [], 192
    corner = 240
    for a, b, c in DIRECTIONS:
        steps = [step for step in (a, b, c) if step]
        if steps[0] < 0:
            continue
        if len(steps) == 1:
            listed.append(((a, b, c), 64 * (0 if a else (1 if b else 2)), 64))
        elif len(steps) == 2:
            listed.append(((a, b, c), begin, 8))
            begin += 8
        else:
            listed.append(((a, b, c), corner, 1))
            corner += 1
    return listed


RIM_ROWS = 248
SENT = (4, 3, -3, 2, -2, 1, -1)


def face_rows(offsets):
    a, b, c = offsets
    y_at, z_at = (7 if b < 0 else 0), (7 if c < 0 else 0)
    if a:
        if b == 0:
            return pl.ds(0, 64) if c == 0 else pl.ds(z_at, 8, stride=8)
        return pl.ds(8 * y_at, 8) if c == 0 else pl.ds(8 * y_at + z_at, 1)
    if b:
        return pl.ds(64, 64) if c == 0 else pl.ds(64 + z_at, 8, stride=8)
    return pl.ds(128, 64)


def plan_kernel(place, own_table, other_table, plan):
    core, low_x, depth = place[0], place[1], place[2]
    for peer in range(4):
        table = other_table if peer & 1 else own_table
        slot = core ^ (peer >> 1)
        for number in range(26):
            entry = table[slot, number]
            here = (entry >= 0) & ((entry & 1) == core) & (((entry >> 1) & 1) == low_x)
            plan[peer, number] = jnp.where(here, (depth - (entry >> 2)) & 7, -1)


def make_plan(place, own_table, other_table):
    return call(plan_kernel, arr((4, 26), jnp.int32))(in_specs=[SMEM, SMEM, SMEM], out_specs=SMEM)(
        place, own_table, other_table
    )


def rims_kernel(plan, *rest):
    blocks, outs, gathered = rest[:8], rest[8:12], rest[12]
    for number, step in enumerate(SENT + (0,)):
        gathered[step % 8] = blocks[number][...]
    for peer in range(4):
        out = outs[peer]
        out[240:248, :] = jnp.zeros((8, 128), F32)

        def load(offsets):
            index = plan[peer, DIRECTIONS.index(offsets)]
            value = gathered[jnp.maximum(index, 0), face_rows(offsets), :]
            return jnp.where(index >= 0, value, 0.0)

        for offsets, begin, count in rim_list():
            up, down = load(offsets), load(tuple(-step for step in offsets))
            lane = lax.broadcasted_iota(jnp.int32, (count, 128), 1)
            out[begin : begin + count, :] = jnp.where(lane < 64, up, down)


def cut_rims(plan, blocks):
    outs = tuple(close((RIM_ROWS, 128)) for _ in range(4))
    return call(rims_kernel, outs, [pltpu.VMEM((8, 192, 128), F32)], touched=1000000)(
        in_specs=[SMEM] + [VMEM] * 8, out_specs=tuple([VMEM] * 4)
    )(plan, *near(blocks))


def fill_rims(rims, padded, columns, after):
    def at(x, y):
        return (x * 10 + y) * ROWS

    for upward, begin, count in rim_list():
        for sign in (1, -1):
            a, b, c = (sign * step for step in upward)
            side = 0 if sign > 0 else 64
            value = rims[begin : begin + count, side : side + 64]
            px, py = {-1: 0, 1: 9}.get(a), {-1: 0, 1: 9}.get(b)
            row = {-1: 7, 0: 8, 1: 16}[c]
            if count == 64:
                for n in range(8):
                    piece = value[8 * n : 8 * n + 8]
                    if a:
                        padded[pl.ds(at(px, 1 + n) + 8, 8), :] = piece
                    elif b:
                        padded[pl.ds(at(1 + n, py) + 8, 8), :] = piece
                    else:
                        begins = ((1 + n) * 10 + 1) * 8
                        if c < 0:
                            where = pl.ds(begins, 8, stride=8)
                            lane = lax.broadcasted_iota(jnp.int32, (8, 128), 1)
                            wide = jnp.concatenate([piece, piece], axis=1)
                            columns[where, :] = jnp.where(lane < 64, wide, columns[where, :])
                        else:
                            after[pl.ds(begins + 7, 8, stride=8), :] = piece
            elif count == 1:
                padded[pl.ds(at(px, py) + row, 1), :] = value
            elif c == 0:
                padded[pl.ds(at(px, py) + 8, 8), :] = value
            elif a:
                padded[pl.ds(at(px, 1) + row, 8, stride=ROWS), :] = value
            else:
                padded[pl.ds(at(1, py) + row, 8, stride=10 * ROWS), :] = value


def lay_out(padded, begin, columns, after, row):
    before = padded[pl.ds(begin + 7, 8), :]
    same = padded[pl.ds(begin + 8, 8), :]
    columns[row : row + 8, :] = jnp.concatenate([before, same], axis=1)
    after[row : row + 8, :] = padded[pl.ds(begin + 9, 8), :]


def center_kernel(rows, center, center_after, padded):
    center[...] = jnp.zeros(center.shape, F32)
    center_after[...] = jnp.zeros(center_after.shape, F32)
    padded[...] = jnp.zeros(padded.shape, F32)
    for spot in range(64):
        padded[pl.ds(spot * ROWS + 8, 8), :] = rows[8 * spot : 8 * spot + 8, :]
    for spot in range(64):
        lay_out(padded, spot * ROWS, center, center_after, ((1 + spot // 8) * 10 + 1 + spot % 8) * 8)


def make_center(rows):
    return call(center_kernel, (close((800, 128)), close((800, 64))), [pltpu.VMEM((64 * ROWS, 64), F32)])(
        in_specs=[VMEM], out_specs=(VMEM, VMEM)
    )(*near([rows]))


def conv_kernel(place, center, center_after, *rest):
    pieces = rest[:4]
    stacked = rest[4]
    outs = rest[5:13]
    rims, padded, columns, after, total, turned = rest[13:]
    rims[...] = (pieces[0][...] + pieces[1][...]) + (pieces[2][...] + pieces[3][...])
    columns[...] = center[...]
    after[...] = center_after[...]
    fill_rims(rims, padded, columns, after)
    for spot in range(100):
        if spot // 10 in (0, 9) or spot % 10 in (0, 9):
            lay_out(padded, spot * ROWS, columns, after, spot * 8)
    for p in range(3):
        firsts, pairs, tails = [], [], []
        for q in range(3):
            begins = [((p + x) * 10 + q) * 8 for x in range(8)]
            values = jnp.concatenate([columns[begin : begin + 64, :] for begin in begins], axis=0)
            ending = jnp.concatenate([after[begin : begin + 64, :] for begin in begins], axis=0)
            top, last = values.astype(BF16).astype(F32), ending.astype(BF16).astype(F32)
            firsts += [top, values - top, top]
            pairs.append(jnp.concatenate([last, ending - last], axis=1))
            tails.append(last)
        ends = [jnp.concatenate(tails[:2], axis=1), tails[2]]
        left = jnp.concatenate([piece.astype(BF16) for piece in firsts + pairs + ends], axis=1)
        sums = jnp.dot(left, stacked[p], preferred_element_type=F32)
        if p == 0:
            total[...] = sums
        else:
            total[...] += sums
    turned[...] = total[...].T
    chip = place[3]
    for step, (along, across) in enumerate(ROUTES + ((0, 0),)):
        target = (((chip >> 1) + along) & 3) * 2 + ((chip & 1) ^ across)
        outs[step][...] = turned[pl.ds(pl.multiple_of(target * 64, 64), 64), :]


def conv(place, center, rims, stacked):
    outs = tuple(close((64, 512)) for _ in range(8))
    scratch = [
        pltpu.VMEM((RIM_ROWS, 128), F32),
        pltpu.VMEM((100 * ROWS, 64), F32),
        pltpu.VMEM((800, 128), F32),
        pltpu.VMEM((800, 64), F32),
        pltpu.VMEM((512, 512), F32),
        pltpu.VMEM((512, 512), F32),
    ]
    return call(
        conv_kernel, outs, scratch, flops=2 * 3 * 1024 * 1728 * 256, touched=8000000, room=24
    )(
        in_specs=[SMEM] + [VMEM] * 7, out_specs=tuple([VMEM] * 8)
    )(place, *near([*center, *rims, stacked]))


def to_other_core(value):
    return lax.ppermute(value, "chan", [(i, i ^ 1) for i in range(16)])


def to_other_x(value):
    return lax.ppermute(value, "leaf", [(i, i ^ 1) for i in range(16)])


def to_other_both(value):
    pairs = [(16 * i + j, 16 * (i ^ 1) + (j ^ 1)) for i in range(16) for j in range(16)]
    return lax.ppermute(value, ("leaf", "chan"), pairs)


def gather_rims(plan, faces, ready):
    found = []
    for step in SENT:
        found.append(lax.ppermute(faces, "leaf", [(i, (i + 2 * step) % 16) for i in range(16)]))
    found, ready, plan = lax.optimization_barrier((found, ready, plan))
    own, beside, across, both = cut_rims(plan, found + [faces])
    return [own, to_other_both(both), to_other_x(beside), to_other_core(across)], ready


def conv_beside(place, center, rims, weights, moved):
    rims, moved = lax.optimization_barrier((rims, moved))
    parts = conv(place, center, rims, weights)
    return lax.optimization_barrier((parts, [to_other_core(value) for value in moved]))


ROUTES = ((2, 1), (1, 1), (3, 1), (2, 0), (0, 1), (1, 0), (3, 0))


def route_target(device, route):
    return (device // 4 + route[0]) % 4 * 4 + ((device % 4) ^ (2 * route[1]))


def add_over_chips(parts):
    landed = [parts[7]]
    for part, route in zip(parts, ROUTES):
        landed.append(lax.ppermute(part, "chan", [(i, route_target(i, route)) for i in range(16)]))
    return landed


def body(features, leaf_counts, occupancy, neighbours, weight_in, bias_in, weight_out, bias_out):
    leaf, chan = lax.axis_index("leaf"), lax.axis_index("chan")
    core = chan % 2
    place = jnp.stack([core, leaf % 2, leaf // 2, chan // 2]).astype(jnp.int32)
    place, weight_in = lax.optimization_barrier((place, weight_in))
    others = to_other_core(features)
    masked, active = call(own_kernel, (close((32, 512)), close((1, 512))))(
        in_specs=[SMEM, SMEM, VMEM, VMEM], out_specs=(VMEM, VMEM)
    )(place, leaf_counts, occupancy, features)
    rows, faces = call(features_kernel, (close((512, 64)), close((192, 128))))(
        in_specs=[SMEM, VMEM, VMEM, VMEM], out_specs=(VMEM, VMEM)
    )(place, *near([masked, active, others]))
    tables = neighbours, to_other_x(neighbours)
    bias_in, bias_out = bias_in.reshape(1, 32), bias_out.reshape(1, 32)
    swapped, tables = lax.optimization_barrier((to_other_core(weight_in), tables))
    weights = split_weights(place, weight_in, swapped)

    plan = make_plan(place, *tables)
    rims, (weights, center) = gather_rims(plan, faces, (weights, make_center(rows)))
    parts, (swapped, other_bias) = conv_beside(place, center, rims, weights, [weight_out, bias_in])
    weights = split_weights(place, weight_out, swapped)
    parts = add_over_chips(parts)
    rows, faces = call(hidden_kernel, (close((512, 64)), close((192, 128))))(
        in_specs=[SMEM, SMEM] + [VMEM] * 11, out_specs=(VMEM, VMEM)
    )(place, leaf_counts, occupancy, bias_in, other_bias, *near(parts))

    rims, center = gather_rims(plan, faces, make_center(rows))
    parts, (other_bias,) = conv_beside(place, center, rims, weights, [bias_out])
    parts = add_over_chips(parts)
    keep, give = call(result_kernel, (close((32, 512)), close((32, 512))))(
        in_specs=[SMEM, SMEM] + [VMEM] * 11, out_specs=(VMEM, VMEM)
    )(place, leaf_counts, occupancy, bias_out, other_bias, *near(parts))
    return call(merge_kernel, arr((32, 2, 512)))(in_specs=[SMEM, VMEM, VMEM], out_specs=VMEM)(
        place, *near([keep, to_other_core(give)])
    )


def solution(mesh):
    placed = (
        P("chan", "leaf", None),
        P("leaf"),
        P("leaf", None),
        P("leaf", None),
        P(None, "chan", None),
        P("chan"),
        P(None, "chan", None),
        P("chan"),
    )
    return jax.shard_map(
        body, mesh=mesh, in_specs=placed, out_specs=P("chan", "leaf", None), check_vma=False
    )
```

```python
import functools

import jax
import jax.numpy as jnp
from jax import lax
from jax.experimental import pallas as pl
from jax.experimental.pallas import tpu as pltpu
from jax.sharding import PartitionSpec as P

DIRECTIONS = [
    (first, second, third)
    for first in (-1, 0, 1)
    for second in (-1, 0, 1)
    for third in (-1, 0, 1)
    if (first, second, third) != (0, 0, 0)
]
VMEM = pl.BlockSpec(memory_space=pltpu.VMEM)
SMEM = pl.BlockSpec(memory_space=pltpu.SMEM)
F32 = jnp.float32
BF16 = jnp.bfloat16
ROWS = 24


def call(kernel, outs, scratch=(), flops=1000000, touched=1000000, room=16):
    return functools.partial(
        pl.pallas_call,
        kernel,
        out_shape=outs,
        scratch_shapes=list(scratch),
        compiler_params=pltpu.CompilerParams(vmem_limit_bytes=room * 1024 * 1024),
        cost_estimate=pl.CostEstimate(flops=flops, bytes_accessed=touched, transcendentals=0),
    )


def arr(shape, dtype=F32):
    return jax.ShapeDtypeStruct(shape, dtype)


def close(shape, dtype=F32):
    return pltpu.VMEM(shape, dtype)


def near(values):
    return [pltpu.with_memory_space_constraint(value, pltpu.VMEM) for value in values]


DEPTH = 3 * 9 * 64


def weights_kernel(place, own, other, stacked):
    core = place[0]
    for tap in range(27):
        p, q, r = tap // 9, tap // 3 % 3, tap % 3
        both = in_order(core, own[tap], other[tap])
        top = both.astype(BF16)
        low = (both - top.astype(F32)).astype(BF16)
        if r < 2:
            begin = 384 * q + 64 * r
            rows = (begin, begin + 128, begin + 256)
        else:
            rows = (1152 + 128 * q, 1216 + 128 * q, 1536 + 64 * q)
        for row, value in zip(rows, (top, top, low)):
            stacked[p, row : row + 64, :] = value


def split_weights(place, own, other):
    return call(weights_kernel, close((3, DEPTH, 512), BF16), flops=8000000, touched=9000000)(
        in_specs=[SMEM, VMEM, VMEM], out_specs=VMEM
    )(place, own, other)


def cut_faces(rows, faces):
    faces[0:64, :] = jnp.concatenate([rows[0:64, :], rows[448:512, :]], axis=1)
    for x in range(8):
        faces[64 + 8 * x : 72 + 8 * x, :] = jnp.concatenate(
            [rows[64 * x : 64 * x + 8, :], rows[64 * x + 56 : 64 * x + 64, :]], axis=1
        )
    faces[128:192, :] = jnp.concatenate(
        [rows[pl.ds(0, 64, stride=8), :], rows[pl.ds(7, 64, stride=8), :]], axis=1
    )


def in_order(core, own, other):
    first = jnp.where(core == 0, own, other)
    second = jnp.where(core == 0, other, own)
    return jnp.concatenate([first, second], axis=0)


def active_voxels(core, counts, occupancy):
    chosen = jnp.where(core == 0, occupancy[0:1, :], occupancy[1:2, :]).astype(F32)
    return chosen * jnp.where(core < counts[0], 1.0, 0.0)


def own_kernel(place, counts, occupancy, own, masked, active):
    core = place[0]
    active[...] = active_voxels(core, counts, occupancy)
    masked[...] = jnp.where(core == 0, own[:, 0, :], own[:, 1, :]) * active[...]


def features_kernel(place, masked, active, other, rows, faces):
    core = place[0]
    theirs = jnp.where(core == 0, other[:, 0, :], other[:, 1, :]) * active[...]
    rows[...] = in_order(core, masked[...], theirs).T
    cut_faces(rows, faces)


def added(parts):
    value = parts[0][...]
    for part in parts[1:]:
        value = value + part[...]
    return value


def bias_row(core, own_bias, other_bias):
    own, other = own_bias[...], other_bias[...]
    first = jnp.where(core == 0, own, other)
    second = jnp.where(core == 0, other, own)
    return jnp.concatenate([first, second], axis=1)


def bias_column(row):
    wide = jnp.concatenate([row, row], axis=1)
    return jnp.broadcast_to(wide, (128, 128)).T[0:64, 0:1]


def hidden_kernel(place, counts, occupancy, own_bias, other_bias, *rest):
    core = place[0]
    rows, faces = rest[8:]
    bias = bias_column(bias_row(core, own_bias, other_bias))
    value = jnp.maximum(added(rest[:8]) + bias, 0.0)
    rows[...] = (value * active_voxels(core, counts, occupancy)).T
    cut_faces(rows, faces)


def result_kernel(place, counts, occupancy, own_bias, other_bias, *rest):
    core = place[0]
    keep, give = rest[8:]
    bias = bias_column(bias_row(core, own_bias, other_bias))
    value = (added(rest[:8]) + bias) * active_voxels(core, counts, occupancy)
    keep[...] = jnp.where(core == 0, value[0:32], value[32:64])
    give[...] = jnp.where(core == 0, value[32:64], value[0:32])


def merge_kernel(place, keep, got, out):
    core = place[0]
    out[:, 0, :] = jnp.where(core == 0, keep[...], got[...])
    out[:, 1, :] = jnp.where(core == 0, got[...], keep[...])


def rim_list():
    listed, begin = [], 192
    corner = 240
    for a, b, c in DIRECTIONS:
        steps = [step for step in (a, b, c) if step]
        if steps[0] < 0:
            continue
        if len(steps) == 1:
            listed.append(((a, b, c), 64 * (0 if a else (1 if b else 2)), 64))
        elif len(steps) == 2:
            listed.append(((a, b, c), begin, 8))
            begin += 8
        else:
            listed.append(((a, b, c), corner, 1))
            corner += 1
    return listed


RIM_ROWS = 248
SENT = (-1, 1, -2, 2, -3, 3, 4)


def face_rows(offsets):
    a, b, c = offsets
    y_at, z_at = (7 if b < 0 else 0), (7 if c < 0 else 0)
    if a:
        if b == 0:
            return pl.ds(0, 64) if c == 0 else pl.ds(z_at, 8, stride=8)
        return pl.ds(8 * y_at, 8) if c == 0 else pl.ds(8 * y_at + z_at, 1)
    if b:
        return pl.ds(64, 64) if c == 0 else pl.ds(64 + z_at, 8, stride=8)
    return pl.ds(128, 64)


def plan_kernel(place, own_table, other_table, plan):
    core, low_x, depth = place[0], place[1], place[2]
    for peer in range(4):
        table = other_table if peer & 1 else own_table
        slot = core ^ (peer >> 1)
        for number in range(26):
            entry = table[slot, number]
            here = (entry >= 0) & ((entry & 1) == core) & (((entry >> 1) & 1) == low_x)
            plan[peer, number] = jnp.where(here, (depth - (entry >> 2)) & 7, -1)


def make_plan(place, own_table, other_table):
    return call(plan_kernel, arr((4, 26), jnp.int32))(in_specs=[SMEM, SMEM, SMEM], out_specs=SMEM)(
        place, own_table, other_table
    )


def rims_kernel(plan, *rest):
    blocks, outs, gathered = rest[:8], rest[8:12], rest[12]
    for number, step in enumerate(SENT + (0,)):
        gathered[step % 8] = blocks[number][...]
    for peer in range(4):
        out = outs[peer]
        out[240:248, :] = jnp.zeros((8, 128), F32)

        def load(offsets):
            index = plan[peer, DIRECTIONS.index(offsets)]
            value = gathered[jnp.maximum(index, 0), face_rows(offsets), :]
            return jnp.where(index >= 0, value, 0.0)

        for offsets, begin, count in rim_list():
            up, down = load(offsets), load(tuple(-step for step in offsets))
            lane = lax.broadcasted_iota(jnp.int32, (count, 128), 1)
            out[begin : begin + count, :] = jnp.where(lane < 64, up, down)


def cut_rims(plan, blocks):
    outs = tuple(close((RIM_ROWS, 128)) for _ in range(4))
    return call(rims_kernel, outs, [pltpu.VMEM((8, 192, 128), F32)], touched=1000000)(
        in_specs=[SMEM] + [VMEM] * 8, out_specs=tuple([VMEM] * 4)
    )(plan, *near(blocks))


def fill_rims(rims, padded, columns, after):
    def at(x, y):
        return (x * 10 + y) * ROWS

    for upward, begin, count in rim_list():
        for sign in (1, -1):
            a, b, c = (sign * step for step in upward)
            side = 0 if sign > 0 else 64
            value = rims[begin : begin + count, side : side + 64]
            px, py = {-1: 0, 1: 9}.get(a), {-1: 0, 1: 9}.get(b)
            row = {-1: 7, 0: 8, 1: 16}[c]
            if count == 64:
                for n in range(8):
                    piece = value[8 * n : 8 * n + 8]
                    if a:
                        padded[pl.ds(at(px, 1 + n) + 8, 8), :] = piece
                    elif b:
                        padded[pl.ds(at(1 + n, py) + 8, 8), :] = piece
                    else:
                        begins = ((1 + n) * 10 + 1) * 8
                        if c < 0:
                            where = pl.ds(begins, 8, stride=8)
                            lane = lax.broadcasted_iota(jnp.int32, (8, 128), 1)
                            wide = jnp.concatenate([piece, piece], axis=1)
                            columns[where, :] = jnp.where(lane < 64, wide, columns[where, :])
                        else:
                            after[pl.ds(begins + 7, 8, stride=8), :] = piece
            elif count == 1:
                padded[pl.ds(at(px, py) + row, 1), :] = value
            elif c == 0:
                padded[pl.ds(at(px, py) + 8, 8), :] = value
            elif a:
                padded[pl.ds(at(px, 1) + row, 8, stride=ROWS), :] = value
            else:
                padded[pl.ds(at(1, py) + row, 8, stride=10 * ROWS), :] = value


def lay_out(padded, begin, columns, after, row):
    before = padded[pl.ds(begin + 7, 8), :]
    same = padded[pl.ds(begin + 8, 8), :]
    columns[row : row + 8, :] = jnp.concatenate([before, same], axis=1)
    after[row : row + 8, :] = padded[pl.ds(begin + 9, 8), :]


def center_kernel(rows, center, center_after, padded):
    center[...] = jnp.zeros(center.shape, F32)
    center_after[...] = jnp.zeros(center_after.shape, F32)
    padded[...] = jnp.zeros(padded.shape, F32)
    for spot in range(64):
        padded[pl.ds(spot * ROWS + 8, 8), :] = rows[8 * spot : 8 * spot + 8, :]
    for spot in range(64):
        lay_out(padded, spot * ROWS, center, center_after, ((1 + spot // 8) * 10 + 1 + spot % 8) * 8)


def make_center(rows):
    return call(center_kernel, (close((800, 128)), close((800, 64))), [pltpu.VMEM((64 * ROWS, 64), F32)])(
        in_specs=[VMEM], out_specs=(VMEM, VMEM)
    )(*near([rows]))


def conv_kernel(place, center, center_after, *rest):
    pieces = rest[:4]
    stacked = rest[4]
    outs = rest[5:13]
    rims, padded, columns, after, total, turned = rest[13:]
    rims[...] = (pieces[0][...] + pieces[1][...]) + (pieces[2][...] + pieces[3][...])
    columns[...] = center[...]
    after[...] = center_after[...]
    fill_rims(rims, padded, columns, after)
    for spot in range(100):
        if spot // 10 in (0, 9) or spot % 10 in (0, 9):
            lay_out(padded, spot * ROWS, columns, after, spot * 8)
    for p in range(3):
        firsts, pairs, tails = [], [], []
        for q in range(3):
            begins = [((p + x) * 10 + q) * 8 for x in range(8)]
            values = jnp.concatenate([columns[begin : begin + 64, :] for begin in begins], axis=0)
            ending = jnp.concatenate([after[begin : begin + 64, :] for begin in begins], axis=0)
            top, last = values.astype(BF16).astype(F32), ending.astype(BF16).astype(F32)
            firsts += [top, values - top, top]
            pairs.append(jnp.concatenate([last, ending - last], axis=1))
            tails.append(last)
        ends = [jnp.concatenate(tails[:2], axis=1), tails[2]]
        left = jnp.concatenate([piece.astype(BF16) for piece in firsts + pairs + ends], axis=1)
        sums = jnp.dot(left, stacked[p], preferred_element_type=F32)
        if p == 0:
            total[...] = sums
        else:
            total[...] += sums
    turned[...] = total[...].T
    chip = place[3]
    for step, (along, across) in enumerate(ROUTES + ((0, 0),)):
        target = (((chip >> 1) + along) & 3) * 2 + ((chip & 1) ^ across)
        outs[step][...] = turned[pl.ds(pl.multiple_of(target * 64, 64), 64), :]


def conv(place, center, rims, stacked):
    outs = tuple(close((64, 512)) for _ in range(8))
    scratch = [
        pltpu.VMEM((RIM_ROWS, 128), F32),
        pltpu.VMEM((100 * ROWS, 64), F32),
        pltpu.VMEM((800, 128), F32),
        pltpu.VMEM((800, 64), F32),
        pltpu.VMEM((512, 512), F32),
        pltpu.VMEM((512, 512), F32),
    ]
    return call(
        conv_kernel, outs, scratch, flops=2 * 3 * 1024 * 1728 * 256, touched=8000000, room=24
    )(
        in_specs=[SMEM] + [VMEM] * 7, out_specs=tuple([VMEM] * 8)
    )(place, *near([*center, *rims, stacked]))


def to_other_core(value):
    return lax.ppermute(value, "chan", [(i, i ^ 1) for i in range(16)])


def to_other_x(value):
    return lax.ppermute(value, "leaf", [(i, i ^ 1) for i in range(16)])


def to_other_both(value):
    pairs = [(16 * i + j, 16 * (i ^ 1) + (j ^ 1)) for i in range(16) for j in range(16)]
    return lax.ppermute(value, ("leaf", "chan"), pairs)


def gather_rims(plan, faces, ready):
    found = []
    for step in SENT:
        found.append(lax.ppermute(faces, "leaf", [(i, (i + 2 * step) % 16) for i in range(16)]))
    found, ready, plan = lax.optimization_barrier((found, ready, plan))
    own, beside, across, both = cut_rims(plan, found + [faces])
    return [own, to_other_both(both), to_other_x(beside), to_other_core(across)], ready


def conv_beside(place, center, rims, weights, moved):
    rims, moved, weights = lax.optimization_barrier((rims, moved, weights))
    parts = conv(place, center, rims, weights)
    return lax.optimization_barrier((parts, [to_other_core(value) for value in moved]))


ROUTES = ((2, 1), (1, 1), (3, 1), (2, 0), (0, 1), (1, 0), (3, 0))


def route_target(device, route):
    return (device // 4 + route[0]) % 4 * 4 + ((device % 4) ^ (2 * route[1]))


def add_over_chips(parts):
    landed = [parts[7]]
    for part, route in zip(parts, ROUTES):
        landed.append(lax.ppermute(part, "chan", [(i, route_target(i, route)) for i in range(16)]))
    return landed


def body(features, leaf_counts, occupancy, neighbours, weight_in, bias_in, weight_out, bias_out):
    leaf, chan = lax.axis_index("leaf"), lax.axis_index("chan")
    core = chan % 2
    place = jnp.stack([core, leaf % 2, leaf // 2, chan // 2]).astype(jnp.int32)
    place, weight_in = lax.optimization_barrier((place, weight_in))
    others = to_other_core(features)
    masked, active = call(own_kernel, (close((32, 512)), close((1, 512))))(
        in_specs=[SMEM, SMEM, VMEM, VMEM], out_specs=(VMEM, VMEM)
    )(place, leaf_counts, occupancy, features)
    rows, faces = call(features_kernel, (close((512, 64)), close((192, 128))))(
        in_specs=[SMEM, VMEM, VMEM, VMEM], out_specs=(VMEM, VMEM)
    )(place, *near([masked, active, others]))
    tables = neighbours, to_other_x(neighbours)
    bias_in, bias_out = bias_in.reshape(1, 32), bias_out.reshape(1, 32)
    swapped, tables = lax.optimization_barrier((to_other_core(weight_in), tables))
    weights = split_weights(place, weight_in, swapped)

    plan = make_plan(place, *tables)
    rims, center = gather_rims(plan, faces, make_center(rows))
    parts, (swapped, other_bias) = conv_beside(place, center, rims, weights, [weight_out, bias_in])
    weights = split_weights(place, weight_out, swapped)
    parts = add_over_chips(parts)
    rows, faces = call(hidden_kernel, (close((512, 64)), close((192, 128))))(
        in_specs=[SMEM, SMEM] + [VMEM] * 11, out_specs=(VMEM, VMEM)
    )(place, leaf_counts, occupancy, bias_in, other_bias, *near(parts))

    rims, center = gather_rims(plan, faces, make_center(rows))
    parts, (other_bias,) = conv_beside(place, center, rims, weights, [bias_out])
    parts = add_over_chips(parts)
    keep, give = call(result_kernel, (close((32, 512)), close((32, 512))))(
        in_specs=[SMEM, SMEM] + [VMEM] * 11, out_specs=(VMEM, VMEM)
    )(place, leaf_counts, occupancy, bias_out, other_bias, *near(parts))
    return call(merge_kernel, arr((32, 2, 512)))(in_specs=[SMEM, VMEM, VMEM], out_specs=VMEM)(
        place, *near([keep, to_other_core(give)])
    )


def solution(mesh):
    placed = (
        P("chan", "leaf", None),
        P("leaf"),
        P("leaf", None),
        P("leaf", None),
        P(None, "chan", None),
        P("chan"),
        P(None, "chan", None),
        P("chan"),
    )
    return jax.shard_map(
        body, mesh=mesh, in_specs=placed, out_specs=P("chan", "leaf", None), check_vma=False
    )
```
